32 devices in a mesh: section: 4 (over z), seq: 8 (over y, x, core).
Axes of the slice: x: 2, y: 2, z: 4, core: 2. Of those that a mesh axis runs over, the one named last changes fastest.
Arguments:
- inbound_embedding_batches: bfloat16 [2, 128, 4096], replicated, may hold values from -16 to 16
- decoder_embedding_batches: bfloat16 [2, 128, 4096], replicated, may hold values from -16 to 16
- asking_projections: bfloat16 [4, 4096, 4096], P('section', None, 'seq'), may hold values from -0.09375 to 0.09375
- probe_projections: bfloat16 [4, 4096, 4096], P('section', None, 'seq'), may hold values from -0.09375 to 0.09375
- payload_projections: bfloat16 [4, 4096, 4096], P('section', None, 'seq'), may hold values from -0.09375 to 0.09375
- exit_projections: bfloat16 [4, 4096, 4096], P('section', 'seq'), may hold values from -0.1875 to 0.1875
- layer_rescale_weights: float32 [4, 4096], P('section'), may hold values from 0.1 to 1.9
- logit_sharpness: float32 [4, 64], P('section', 'seq'), may hold values from 0.5 to 3
- last_rescale_weights: float32 [4096], replicated, may hold values from 0.1 to 1.9
Outputs:
- section_out: bfloat16 [4, 2, 128, 4096], P('section')
The draws below stay inside these ranges and needn't reach their ends.
All inputs are finite; a program needn't handle non-finite values.
Results may differ from the reference program's by a relative error of at most 0.025.
Values may be sent and summed in bfloat16 or wider, within the bound.
No kernel may reach another device: no remote copies, remote signals or barrier semaphores. Data moves between devices by JAX's collectives and lax.ppermute only.
A program may use at most 64 MiB of HBM per device.

```python
import math
import jax
import jax.numpy as jnp
from jax import lax

D = 4096
NUM_HEADS = 64
LENGTH = 128
MICRO = 2
INNER = 4096
ENC_SECTIONS = 1
N_SECTION = 4
N_SEQ = 8


def scaled_embeddings(key):
    first_key, second_key, third_key = jax.random.split(key, 3)
    base = jax.random.normal(first_key, (MICRO, LENGTH, D), jnp.float32)
    base = jnp.clip(base, -4.0, 4.0)
    row_scale = jnp.exp(jax.random.uniform(second_key, (MICRO, LENGTH, 1), jnp.float32, math.log(0.2), math.log(2.0)))
    column_scale = jnp.exp(jax.random.uniform(third_key, (1, 1, D), jnp.float32, math.log(0.5), math.log(2.0)))
    return base * row_scale * column_scale


def draw_inbound_embedding_batches(key, part):
    return scaled_embeddings(jax.random.fold_in(key, 11)).astype(jnp.bfloat16)


def draw_decoder_embedding_batches(key, part):
    return scaled_embeddings(jax.random.fold_in(key, 23)).astype(jnp.bfloat16)


def levels(stream_key, shape, shards, least, high):
    def one(position, parts):
        heights = jax.random.uniform(jax.random.fold_in(jax.random.fold_in(stream_key, 6), position), (parts,), jnp.float32, least / len(shards), high / len(shards))
        return jnp.repeat(jnp.exp(heights), shape[position] // parts).reshape((-1,) + (1,) * (len(shape) - position - 1))

    factor_of = one(*shards[0])
    for cut in shards[1:]:
        factor_of = factor_of * one(*cut)
    return factor_of


def noise(key, shape, deviation, reach, shards=(), held_as=jnp.bfloat16):
    loudness = levels(key, shape, shards, -0.22, 0.18) if shards else 1.0
    entries = jax.random.normal(key, shape, jnp.float32) * deviation * loudness
    return jnp.minimum(jnp.maximum(entries, -reach), reach).astype(held_as)


def setup_inputs(seed: int = 0) -> dict:
    key_of = jax.random.split(jax.random.key(seed), 10)
    inbound_embedding_batches = draw_inbound_embedding_batches(jax.random.fold_in(key_of[9], 71), 0)
    decoder_embedding_batches = draw_decoder_embedding_batches(jax.random.fold_in(key_of[9], 71), 0)
    asking_projections = noise(key_of[2], (N_SECTION, D, INNER), D ** -0.5, 0.09375, ((0, 4), (2, 8)))
    probe_projections = noise(key_of[3], (N_SECTION, D, INNER), D ** -0.5, 0.09375, ((0, 4), (2, 8)))
    payload_projections = noise(key_of[4], (N_SECTION, D, INNER), D ** -0.5, 0.09375, ((0, 4), (2, 8)))
    exit_projections = noise(key_of[5], (N_SECTION, INNER, D), (INNER // 4) ** -0.5, 0.1875, ((0, 4), (1, 8)))
    layer_rescale_weights = jnp.clip(1.0 + 0.18 * jax.random.normal(key_of[6], (N_SECTION, D), jnp.float32), 0.1, 1.9)
    logit_sharpness = jnp.clip(jnp.exp(math.log(3.0) - 1.7917595 * jax.random.uniform(key_of[7], (N_SECTION, NUM_HEADS), jnp.float32) ** levels(key_of[7], (N_SECTION, NUM_HEADS), ((0, 4), (1, 8)), -0.2, 0.2)), 0.5, 3.0)
    last_rescale_weights = jnp.clip(1.0 + 0.18 * jax.random.normal(key_of[8], (D,), jnp.float32), 0.1, 1.9)
    return dict(inbound_embedding_batches=inbound_embedding_batches, decoder_embedding_batches=decoder_embedding_batches, asking_projections=asking_projections, probe_projections=probe_projections, payload_projections=payload_projections, exit_projections=exit_projections, layer_rescale_weights=layer_rescale_weights, logit_sharpness=logit_sharpness, last_rescale_weights=last_rescale_weights)


epsilon = 1e-06

def normalize(row_block, gain_vector):
    values = row_block.astype(jnp.float32)
    factor = lax.rsqrt(lax.optimization_barrier(jnp.mean(values * values, axis=-1, keepdims=True)) + epsilon)
    return (values * factor * gain_vector).astype(jnp.bfloat16)

def unit_heads(projected):
    return (projected * lax.rsqrt(lax.optimization_barrier(jnp.mean(projected * projected, axis=-1, keepdims=True)) + epsilon)).astype(jnp.bfloat16)

def mixed_context(rescaled_activations, context_states, w_query, w_key, w_value, logit_divisor):
    length = rescaled_activations.shape[0]
    head_count = logit_divisor.shape[0]
    head_size = w_query.shape[1] // head_count
    queries = jnp.dot(rescaled_activations, w_query, preferred_element_type=jnp.float32).reshape(length, head_count, head_size)
    keys_proj = jnp.dot(context_states, w_key, preferred_element_type=jnp.float32).reshape(context_states.shape[0], head_count, head_size)
    values_proj = jnp.dot(context_states, w_value, preferred_element_type=jnp.float32).astype(jnp.bfloat16)
    values_proj = values_proj.reshape(context_states.shape[0], head_count, head_size)
    unit_query = unit_heads(queries)
    unit_key = unit_heads(keys_proj)
    scores = jnp.einsum('qhd,khd->hqk', unit_query.astype(jnp.float32), unit_key.astype(jnp.float32), precision=lax.Precision.HIGHEST)
    scores = scores * (logit_divisor.astype(jnp.float32)[:, None, None] / math.sqrt(head_size))
    weights = jnp.exp(scores)
    weights = (weights / lax.optimization_barrier(jnp.sum(weights, axis=-1, keepdims=True))).astype(jnp.bfloat16)
    blended_payloads = jnp.einsum('hqk,khd->qhd', weights.astype(jnp.float32), values_proj.astype(jnp.float32), precision=lax.Precision.HIGHEST)
    return blended_payloads.astype(jnp.bfloat16).reshape(length, head_count * head_size)

def project_out(blended_payloads, w_output):
    block = blended_payloads.shape[1] // N_SEQ
    total = jnp.zeros((blended_payloads.shape[0], w_output.shape[1]), jnp.float32)
    for block_index in range(N_SEQ):
        lower = block_index * block
        partial_term = jnp.dot(blended_payloads[:, lower:lower + block], w_output[lower:lower + block], preferred_element_type=jnp.float32).astype(jnp.bfloat16)
        partial_term = lax.optimization_barrier(partial_term)
        total = total + partial_term.astype(jnp.float32)
    return total

def reference(inbound_embedding_batches, decoder_embedding_batches, asking_projections, probe_projections, payload_projections, exit_projections, layer_rescale_weights, logit_sharpness, last_rescale_weights):
    table = []
    for present_layer_index in range(N_SECTION):
        table.append([])
    for batch_index in range(MICRO):
        stream = inbound_embedding_batches[batch_index]
        encoded = stream
        for present_layer_index in range(N_SECTION):
            if present_layer_index == ENC_SECTIONS:
                stream = decoder_embedding_batches[batch_index]
            rescaled_activations = normalize(stream, layer_rescale_weights[present_layer_index])
            if present_layer_index < ENC_SECTIONS:
                context_states = rescaled_activations
            else:
                context_states = normalize(encoded, last_rescale_weights)
            blended_payloads = mixed_context(rescaled_activations, context_states, asking_projections[present_layer_index], probe_projections[present_layer_index], payload_projections[present_layer_index], logit_sharpness[present_layer_index])
            update = project_out(blended_payloads, exit_projections[present_layer_index])
            stream = (stream.astype(jnp.float32) + update).astype(jnp.bfloat16)
            table[present_layer_index].append(stream)
            if present_layer_index == ENC_SECTIONS - 1:
                encoded = stream
    return jnp.stack([jnp.stack(column) for column in table])
```

```python
import functools

import jax
import jax.numpy as jnp
from jax import lax
from jax.experimental import pallas as pl
from jax.experimental.pallas import tpu as pltpu
from jax.sharding import PartitionSpec as P

EPSILON = 1e-06
LANES = 128
BF16 = jnp.bfloat16
F32 = jnp.float32
VMEM_LIMIT = 56 * 1024 * 1024
ANY = pl.BlockSpec(memory_space=pl.ANY)
IN_VMEM = pl.BlockSpec(memory_space=pltpu.VMEM)
IN_SMEM = pl.BlockSpec(memory_space=pltpu.SMEM)


def params():
    return pltpu.CompilerParams(vmem_limit_bytes=VMEM_LIMIT)


class Copies:
    def __init__(self, sems):
        self.sems, self.used = sems, 0

    def start(self, src, dst):
        copy = pltpu.make_async_copy(src, dst, self.sems.at[self.used])
        self.used += 1
        copy.start()
        return copy


def normalize_rows(raw, out, gain, rows, step=16):
    def body(i, _):
        at = pl.ds(pl.multiple_of(i * step, step), step)
        values = raw[at, :].astype(F32)
        factor = lax.rsqrt(jnp.mean(values * values, axis=-1, keepdims=True) + EPSILON)
        out[at, :] = (values * factor * gain[...]).astype(BF16)
        return 0

    lax.fori_loop(0, rows // step, body, 0)


def lane_masks(rows, head):
    lane = lax.broadcasted_iota(jnp.int32, (rows, LANES), 1)
    return [(lane // head) == i for i in range(LANES // head)]


def unit(block, head):
    masks = lane_masks(block.shape[0], head)
    squares = block * block
    factor = None
    for mask in masks:
        total = jnp.sum(jnp.where(mask, squares, 0.0), axis=-1, keepdims=True)
        own = lax.rsqrt(total / head + EPSILON)
        factor = own if factor is None else jnp.where(mask, own, factor)
    return (block * factor).astype(BF16)


def attend(queries, keys, values, scales, head):
    rows = queries.shape[0]
    masks = lane_masks(rows, head)
    stacked = jnp.concatenate(
        [jnp.where(mask, queries, jnp.zeros_like(queries)) for mask in masks], axis=0
    )
    scores = lax.dot_general(
        stacked, keys, (((1,), (1,)), ((), ())), preferred_element_type=F32
    )
    weights = []
    for i, scale in enumerate(scales):
        raised = jnp.exp(scores[i * rows : (i + 1) * rows] * scale)
        weights.append((raised / jnp.sum(raised, axis=-1, keepdims=True)).astype(BF16))
    mixed = jnp.dot(jnp.concatenate(weights, axis=0), values, preferred_element_type=F32)
    out = mixed[:rows]
    for i in range(1, len(scales)):
        out = jnp.where(masks[i], mixed[i * rows : (i + 1) * rows], out)
    return out.astype(BF16)


class Weight:
    def __init__(self, copies, sources, scratch, wide):
        self.scratch, self.chunks = scratch, []
        for source in sources:
            for at in range(0, source.shape[1], wide):
                self.chunks.append(
                    copies.start(source.at[:, pl.ds(at, wide)], scratch.at[len(self.chunks)])
                )

    def times(self, rows, chunk):
        self.chunks[chunk].wait()
        return jnp.dot(rows, self.scratch[chunk], preferred_element_type=F32)


class OutWeight:
    def __init__(self, copies, sources, scratch, wide):
        self.scratch, self.wide, self.chunks = scratch, wide, []
        for at in range(0, scratch.shape[1], wide):
            parts, low = [], 0
            for source in sources:
                height = source.shape[0]
                parts.append(
                    copies.start(
                        source.at[:, pl.ds(at, wide)],
                        scratch.at[pl.ds(low, height), pl.ds(at, wide)],
                    )
                )
                low += height
            self.chunks.append(parts)

    def into(self, mixture, outs):
        height = mixture.shape[0] // len(outs)
        for i, parts in enumerate(self.chunks):
            for part in parts:
                part.wait()
            at = pl.ds(i * self.wide, self.wide)
            product = jnp.dot(mixture, self.scratch[:, at], preferred_element_type=F32).astype(BF16)
            for k, out in enumerate(outs):
                out[:, at] = product[k * height : (k + 1) * height]


def load_rows(copies, source, batch, scratch, low, chip, blocks):
    height = source.shape[1] // blocks
    waits = []
    for j in range(blocks):
        at = pl.multiple_of((chip ^ j) * height, height)
        waits.append(
            copies.start(
                source.at[batch, pl.ds(at, height), :],
                scratch.at[pl.ds(low + j * height, height), :],
            )
        )
    return waits


def load_pieces(copies, pieces, scratch):
    waits, low = [], 0
    for piece in pieces:
        height = piece.shape[0]
        waits.append(copies.start(piece, scratch.at[pl.ds(low, height), :]))
        low += height
    return waits


WIDE = 256
OUT_WIDE = 1024


def first_kernel(config, place, sharp, gain, source, wq, wk, wv, own_ref, other_ref,
                 raw, rows, wq_s, wk_s, wv_s, sems):
    head, blocks, length = config
    copies = Copies(sems)
    chip, core = place[0], place[1]
    waits = load_rows(copies, source, core, raw, 0, chip, blocks)
    waits += load_rows(copies, source, 1 - core, raw, length, chip, blocks)
    weights = [Weight(copies, [w], s, WIDE) for w, s in ((wq, wq_s), (wk, wk_s), (wv, wv_s))]
    for wait in waits:
        wait.wait()
    normalize_rows(raw, rows, gain, raw.shape[0])
    normed = rows[...]
    per = LANES // head
    for chunk in range(wq.shape[1] // WIDE):
        q, k, v = (w.times(normed, chunk) for w in weights)
        v = v.astype(BF16)
        for g in range(WIDE // LANES):
            lanes = slice(g * LANES, (g + 1) * LANES)
            group = chunk * (WIDE // LANES) + g
            scales = [sharp[group * per + i] for i in range(per)]
            uq, uk = unit(q[:, lanes], head), unit(k[:, lanes], head)
            for b, out in enumerate((own_ref, other_ref)):
                at = slice(b * length, (b + 1) * length)
                out[:, group * LANES : (group + 1) * LANES] = attend(
                    uq[at], uk[at], v[at, lanes], scales, head
                )


def out_kernel(config, own, other, wo_own, wo_other, *refs):
    outs, (mixture, wo_s, sems) = refs[:-3], refs[-3:]
    copies = Copies(sems)
    waits = [
        copies.start(part, mixture.at[:, pl.ds(i * part.shape[1], part.shape[1])])
        for i, part in enumerate((own, other))
    ]
    weight = OutWeight(copies, (wo_own, wo_other), wo_s, OUT_WIDE)
    for wait in waits:
        wait.wait()
    weight.into(mixture[...], outs)


def query_kernel(config, place, gain, source, wq_own, wq_other, uq_ref, raw, rows, wq_s, sems):
    head, blocks, length = config
    copies = Copies(sems)
    waits = load_rows(copies, source, place[1], raw, 0, place[0], blocks)
    weight = Weight(copies, (wq_own, wq_other), wq_s, WIDE)
    for wait in waits:
        wait.wait()
    normalize_rows(raw, rows, gain, length)
    project_units(rows[...], weight, uq_ref, head)


def project_units(normed, weight, out, head):
    for chunk in range(len(weight.chunks)):
        product = weight.times(normed, chunk)
        for g in range(WIDE // LANES):
            at = chunk * WIDE + g * LANES
            out[:, at : at + LANES] = unit(product[:, g * LANES : (g + 1) * LANES], head)


def memory_kernel(config, count, gain, *refs):
    head, blocks, length = config
    pieces, refs = refs[:count], refs[count:]
    wk_own, wk_other, wv_own, wv_other, uk_ref, v_ref, raw, rows, wk_s, wv_s, sems = refs
    copies = Copies(sems)
    waits = load_pieces(copies, pieces, raw)
    wk = Weight(copies, (wk_own, wk_other), wk_s, WIDE)
    wv = Weight(copies, (wv_own, wv_other), wv_s, WIDE)
    for wait in waits:
        wait.wait()
    normalize_rows(raw, rows, gain, length)
    normed = rows[...]
    project_units(normed, wk, uk_ref, head)
    for chunk in range(len(wv.chunks)):
        v_ref[:, chunk * WIDE : (chunk + 1) * WIDE] = wv.times(normed, chunk).astype(BF16)


def attend_all(uq, uk, v, sharps, mixture, head):
    per = LANES // head
    each = sharps[0].shape[0]
    for group in range(uq.shape[1] // LANES):
        lanes = slice(group * LANES, (group + 1) * LANES)
        scales = []
        for i in range(per):
            index = group * per + i
            scales.append(sharps[index // each][index % each])
        mixture[:, lanes] = attend(uq[:, lanes], uk[:, lanes], v[:, lanes], scales, head)


def mix_kernel(config, sharp_own, sharp_other, uq, uk, v, wo_own, wo_other, *refs):
    head = config[0]
    outs, (mixture, wo_s, sems) = refs[:-3], refs[-3:]
    copies = Copies(sems)
    weight = OutWeight(copies, (wo_own, wo_other), wo_s, OUT_WIDE)
    attend_all(uq, uk, v, (sharp_own, sharp_other), mixture, head)
    weight.into(mixture[...], outs)


def section_kernel(config, count, sharp_own, sharp_other, gain, *refs):
    head, blocks, length = config
    pieces, refs = refs[:count], refs[count:]
    uk, v, wq_own, wq_other, wo_own, wo_other = refs[:6]
    outs, (raw, rows, uq, mixture, wq_s, wo_s, sems) = refs[6:-7], refs[-7:]
    copies = Copies(sems)
    waits = load_pieces(copies, pieces, raw)
    wq = Weight(copies, (wq_own, wq_other), wq_s, WIDE)
    wo = OutWeight(copies, (wo_own, wo_other), wo_s, OUT_WIDE)
    for wait in waits:
        wait.wait()
    normalize_rows(raw, rows, gain, length)
    project_units(rows[...], wq, uq, head)
    attend_all(uq, uk, v, (sharp_own, sharp_other), mixture, head)
    wo.into(mixture[...], outs)


def place_kernel(count, place, *refs):
    pieces, out, sems = refs[:-2], refs[-2], refs[-1]
    copies = Copies(sems)
    chip, core = place[0], place[1]
    waits = []
    for i, piece in enumerate(pieces):
        height = piece.shape[0]
        batch = core if i < count else 1 - core
        at = pl.multiple_of((chip ^ (i % count)) * height, height)
        waits.append(copies.start(piece, out.at[batch, pl.ds(at, height), :]))
    for wait in waits:
        wait.wait()


def shards(
    inbound_embedding_batches,
    decoder_embedding_batches,
    asking_projections,
    probe_projections,
    payload_projections,
    exit_projections,
    layer_rescale_weights,
    logit_sharpness,
    last_rescale_weights,
):
    sections = lax.axis_size("section")
    seq = lax.axis_size("seq")
    section = lax.axis_index("section")
    position = lax.axis_index("seq")
    encoders = 3 * sections // 8
    batches, length, width = inbound_embedding_batches.shape
    cores = 2
    blocks = seq // cores
    assert batches == cores and blocks & (blocks - 1) == 0
    core, chip = position % cores, position // cores
    height = length // blocks
    heads = logit_sharpness.shape[1]
    inner = asking_projections.shape[2]
    head = inner // heads
    both = cores * inner
    config = (head, blocks, length)

    def flip(bits, only_later=False):
        pairs = [(i, i ^ bits) for i in range(seq)]
        if not only_later:
            return lambda x: lax.ppermute(x, "seq", pairs)
        pairs = [(s * seq + a, s * seq + b) for s in range(1, sections) for a, b in pairs]
        return lambda x: lax.ppermute(x, ("section", "seq"), pairs)

    def up(x, source, target):
        return lax.ppermute(x, "section", [(source, target)])

    to_core = flip(1)
    to_chip = [None] + [flip(j * cores) for j in range(1, blocks)]
    later_core = flip(1, only_later=True)

    wq, wk, wv, wo = (
        w[0] for w in (asking_projections, probe_projections, payload_projections, exit_projections)
    )
    gain = layer_rescale_weights
    last_gain = last_rescale_weights.reshape(1, width)
    sharp = logit_sharpness[0] * (head ** -0.5)
    sharp_other = to_core(sharp)
    wo_other = to_core(wo)
    wk_other, wv_other, wq_other = later_core(wk), later_core(wv), later_core(wq)
    place = jnp.stack([chip, core]).astype(jnp.int32)

    def sds(shape, dtype=BF16):
        return jax.ShapeDtypeStruct(shape, dtype)

    def in_chunks(columns):
        return pltpu.VMEM((columns // WIDE, width, WIDE), BF16)

    row_scratch = pltpu.VMEM((length, width), BF16)
    out_scratch = [pltpu.VMEM((length, both), BF16), pltpu.VMEM((both, width), BF16)]
    partials = [sds((height, width))] * blocks
    chunks = both // WIDE
    out_copies = cores * (width // OUT_WIDE)

    def sems(n):
        return pltpu.SemaphoreType.DMA((n,))

    def gather(share):
        return [share] + [to_chip[j](share) for j in range(1, blocks)]

    def finish(parts, residual):
        total = residual.astype(F32) + parts[0].astype(F32)
        for j in range(1, blocks):
            total = total + to_chip[j](parts[j]).astype(F32)
        return total.astype(BF16)

    def own_rows(source):
        return lax.dynamic_slice(source, (core, chip * height, 0), (1, height, width))[0]

    mixed_own, mixed_other = pl.pallas_call(
        functools.partial(first_kernel, config),
        out_shape=[sds((length, inner))] * 2,
        in_specs=[IN_SMEM, IN_SMEM, IN_VMEM, ANY, ANY, ANY, ANY],
        out_specs=[IN_VMEM] * 2,
        scratch_shapes=[
            pltpu.VMEM((batches * length, width), BF16),
            pltpu.VMEM((batches * length, width), BF16),
            in_chunks(inner), in_chunks(inner), in_chunks(inner),
            sems(batches * blocks + 3 * inner // WIDE),
        ],
        compiler_params=params(),
    )(place, sharp, gain, inbound_embedding_batches, wq, wk, wv)
    mixed_other = to_core(mixed_other)
    parts = pl.pallas_call(
        functools.partial(out_kernel, config),
        out_shape=partials,
        in_specs=[ANY] * 4,
        out_specs=[IN_VMEM] * blocks,
        scratch_shapes=out_scratch + [sems(2 + out_copies)],
        compiler_params=params(),
    )(mixed_own, mixed_other, wo, wo_other)
    share = finish(parts, own_rows(inbound_embedding_batches))
    kept = share

    unit_queries = pl.pallas_call(
        functools.partial(query_kernel, config),
        out_shape=sds((length, both)),
        in_specs=[IN_SMEM, IN_VMEM, ANY, ANY, ANY],
        out_specs=IN_VMEM,
        scratch_shapes=[row_scratch, row_scratch, in_chunks(both), sems(blocks + chunks)],
        compiler_params=params(),
    )(place, gain, decoder_embedding_batches, wq, wq_other)

    def project_memory(pieces, scale):
        return pl.pallas_call(
            functools.partial(memory_kernel, config, blocks),
            out_shape=[sds((length, both))] * 2,
            in_specs=[IN_VMEM] + [ANY] * (blocks + 4),
            out_specs=[IN_VMEM] * 2,
            scratch_shapes=[row_scratch, row_scratch, in_chunks(both), in_chunks(both),
                            sems(blocks + 2 * chunks)],
            compiler_params=params(),
        )(scale, *pieces, wk, wk_other, wv, wv_other)

    for step in range(1, sections):
        if step == encoders:
            memory = None
            for target in range(step, sections):
                arrived = up(share, step - 1, target)
                memory = arrived if memory is None else jnp.where(section == target, arrived, memory)
            unit_keys, values = project_memory(gather(memory), last_gain)
            residual = own_rows(decoder_embedding_batches)
            parts = pl.pallas_call(
                functools.partial(mix_kernel, config),
                out_shape=partials,
                in_specs=[IN_SMEM] * 2 + [IN_VMEM] * 3 + [ANY] * 2,
                out_specs=[IN_VMEM] * blocks,
                scratch_shapes=out_scratch + [sems(out_copies)],
                compiler_params=params(),
            )(sharp, sharp_other, unit_queries, unit_keys, values, wo, wo_other)
        else:
            residual = up(share, step - 1, step)
            pieces = gather(residual)
            if step < encoders:
                unit_keys, values = project_memory(pieces, gain)
            parts = pl.pallas_call(
                functools.partial(section_kernel, config, blocks),
                out_shape=partials,
                in_specs=[IN_SMEM] * 2 + [IN_VMEM] + [ANY] * blocks + [IN_VMEM] * 2 + [ANY] * 4,
                out_specs=[IN_VMEM] * blocks,
                scratch_shapes=[
                    row_scratch, row_scratch, pltpu.VMEM((length, both), BF16), out_scratch[0],
                    in_chunks(both), out_scratch[1], sems(blocks + chunks + out_copies),
                ],
                compiler_params=params(),
            )(sharp, sharp_other, gain, *pieces, unit_keys, values, wq, wq_other, wo, wo_other)
        share = finish(parts, residual)
        kept = jnp.where(section == step, share, kept)

    pieces = gather(kept)
    pieces = pieces + [to_core(piece) for piece in pieces]
    finished = pl.pallas_call(
        functools.partial(place_kernel, blocks),
        out_shape=sds((batches, length, width)),
        in_specs=[IN_SMEM] + [ANY] * len(pieces),
        out_specs=ANY,
        scratch_shapes=[sems(len(pieces))],
        compiler_params=params(),
    )(place, *pieces)
    return finished[None]


def solution(mesh):
    return jax.shard_map(
        shards,
        mesh=mesh,
        in_specs=(
            P(),
            P(),
            P("section", None, "seq"),
            P("section", None, "seq"),
            P("section", None, "seq"),
            P("section", "seq", None),
            P("section", None),
            P("section", "seq"),
            P(),
        ),
        out_specs=P("section", None, None, None),
        check_vma=False,
    )
```

```python
import functools

import jax
import jax.numpy as jnp
from jax import lax
from jax.experimental import pallas as pl
from jax.experimental.pallas import tpu as pltpu
from jax.sharding import PartitionSpec as P

EPSILON = 1e-06
LANES = 128
WIDE = 256
OUT_WIDE = 1024
STEP = 16
BF16 = jnp.bfloat16
F32 = jnp.float32
MIB = 1024 * 1024
ANY = pl.BlockSpec(memory_space=pl.ANY)
IN_HBM = pl.BlockSpec(memory_space=pltpu.HBM)
IN_VMEM = pl.BlockSpec(memory_space=pltpu.VMEM)
IN_SMEM = pl.BlockSpec(memory_space=pltpu.SMEM)


def kernel_call(body, outs, ins, scratch, vmem, flops=0, moved=0):
    return pl.pallas_call(
        body,
        out_shape=outs,
        in_specs=ins,
        out_specs=jax.tree.map(lambda _: IN_VMEM, outs),
        scratch_shapes=scratch,
        compiler_params=pltpu.CompilerParams(vmem_limit_bytes=vmem * MIB),
        cost_estimate=pl.CostEstimate(flops=flops, bytes_accessed=moved, transcendentals=0),
    )


class Copies:
    def __init__(self, sems):
        self.sems, self.used = sems, 0

    def start(self, src, dst):
        copy = pltpu.make_async_copy(src, dst, self.sems.at[self.used])
        self.used += 1
        copy.start()
        return copy


def normalize(values, gain):
    values = values.astype(F32)
    factor = lax.rsqrt(jnp.mean(values * values, axis=-1, keepdims=True) + EPSILON)
    return (values * factor * gain).astype(BF16)


def normalize_rows(raw, out, gain):
    def body(i, _):
        at = pl.ds(pl.multiple_of(i * STEP, STEP), STEP)
        out[at, :] = normalize(raw[at, :], gain[...])
        return 0

    lax.fori_loop(0, raw.shape[0] // STEP, body, 0)


def normalize_pieces(pieces, out, gain):
    low = 0
    for piece in pieces:
        height = piece.shape[0]
        out[low : low + height, :] = normalize(piece[...], gain[...])
        low += height


def lane_masks(rows, head):
    lane = lax.broadcasted_iota(jnp.int32, (rows, LANES), 1)
    return [(lane // head) == i for i in range(LANES // head)]


def unit(block, head):
    masks = lane_masks(block.shape[0], head)
    squares = block * block
    factor = None
    for mask in masks:
        total = jnp.sum(jnp.where(mask, squares, 0.0), axis=-1, keepdims=True)
        own = lax.rsqrt(total / head + EPSILON)
        factor = own if factor is None else jnp.where(mask, own, factor)
    return (block * factor).astype(BF16)


def attend(queries, keys, values, scales, head):
    rows = queries.shape[0]
    masks = lane_masks(rows, head)
    stacked = jnp.concatenate(
        [jnp.where(mask, queries, jnp.zeros_like(queries)) for mask in masks], axis=0
    )
    scores = lax.dot_general(
        stacked, keys, (((1,), (1,)), ((), ())), preferred_element_type=F32
    )
    weights = []
    for i, scale in enumerate(scales):
        raised = jnp.exp(scores[i * rows : (i + 1) * rows] * scale)
        weights.append((raised / jnp.sum(raised, axis=-1, keepdims=True)).astype(BF16))
    mixed = jnp.dot(jnp.concatenate(weights, axis=0), values, preferred_element_type=F32)
    out = mixed[:rows]
    for i in range(1, len(scales)):
        out = jnp.where(masks[i], mixed[i * rows : (i + 1) * rows], out)
    return out.astype(BF16)


def attend_all(uq, uk, v, sharps, mixture, head):
    per = LANES // head
    each = sharps[0].shape[0]
    for group in range(uq.shape[1] // LANES):
        lanes = slice(group * LANES, (group + 1) * LANES)
        scales = []
        for i in range(per):
            index = group * per + i
            scales.append(sharps[index // each][index % each])
        mixture[:, lanes] = attend(uq[:, lanes], uk[:, lanes], v[:, lanes], scales, head)


def project(normed, weights, out, finish, wide=WIDE):
    low = 0
    for weight in weights:
        for at in range(0, weight.shape[1], wide):
            product = jnp.dot(normed, weight[:, at : at + wide], preferred_element_type=F32)
            for g in range(0, wide, LANES):
                out[:, low + g : low + g + LANES] = finish(product[:, g : g + LANES])
            low += wide


def project_out(mixture, weights, outs, arrivals=None):
    for at in range(0, weights[0].shape[1], OUT_WIDE):
        for arrival in arrivals[at // OUT_WIDE] if arrivals else ():
            arrival.wait()
        total, low = None, 0
        for weight in weights:
            high = low + weight.shape[0]
            term = jnp.dot(
                mixture[:, low:high], weight[:, at : at + OUT_WIDE], preferred_element_type=F32
            )
            total, low = term if total is None else total + term, high
        total = total.astype(BF16)
        low = 0
        for out in outs:
            out[:, at : at + OUT_WIDE] = total[low : low + out.shape[0]]
            low += out.shape[0]


def load_rows(copies, source, batch, scratch, low, chip, blocks):
    height = source.shape[1] // blocks
    waits = []
    for j in range(blocks):
        at = pl.multiple_of((chip ^ j) * height, height)
        waits.append(
            copies.start(
                source.at[batch, pl.ds(at, height), :],
                scratch.at[pl.ds(low + j * height, height), :],
            )
        )
    return waits


def only_in(sections):
    def wrap(body):
        def wrapped(config, place, *refs):
            here = place[2]
            active = here == sections[0]
            for other in sections[1:]:
                active = active | (here == other)
            pl.when(active)(lambda: body(config, place, *refs))

        return wrapped

    return wrap


def first_kernel(config, place, sharp, gain, source, wq, wk, wv, wo, own_ref, other_ref,
                 raw, rows, wq_s, wk_s, wv_s, wo_s, uq, uk, v, mixture, sems):
    head, blocks, length, _ = config
    copies = Copies(sems)
    chip, core = place[0], place[1]
    waits = load_rows(copies, source, core, raw, 0, chip, blocks)
    waits += load_rows(copies, source, 1 - core, raw, length, chip, blocks)
    weights = [copies.start(w, s) for w, s in ((wq, wq_s), (wk, wk_s), (wv, wv_s))]
    arrivals = stream_out(copies, ((wo, wo_s),))
    for wait in waits:
        wait.wait()
    normalize_rows(raw, rows, gain)
    normed = rows[...]
    wide = wq.shape[1]
    weights[0].wait()
    project(normed, (wq_s,), uq, lambda x: unit(x, head), wide)
    weights[1].wait()
    project(normed, (wk_s,), uk, lambda x: unit(x, head), wide)
    weights[2].wait()
    project(normed, (wv_s,), v, lambda x: x.astype(BF16), wide)
    for low in (0, length):
        at = pl.ds(low, length)
        attend_all(uq[at, :], uk[at, :], v[at, :], (sharp,), mixture.at[at], head)
    project_out(mixture[...], (wo_s,), (own_ref, other_ref), arrivals)


def join_kernel(config, place, own, other, *outs):
    low = 0
    for out in outs:
        at = pl.ds(low, out.shape[0])
        out[...] = (own[at, :].astype(F32) + other[at, :].astype(F32)).astype(BF16)
        low += out.shape[0]


def finish_kernel(config, place, *refs):
    terms, out = refs[:-1], refs[-1]
    total = terms[0][...].astype(F32)
    for term in terms[1:]:
        total = total + term[...].astype(F32)
    out[...] = total.astype(BF16)


def stream_out(copies, pairs):
    arrivals = []
    for at in range(0, pairs[0][0].shape[1], OUT_WIDE):
        columns = pl.ds(at, OUT_WIDE)
        arrivals.append(
            [copies.start(source.at[:, columns], scratch.at[:, columns]) for source, scratch in pairs]
        )
    return arrivals


def query_kernel(config, place, gain, source, wq_own, wq_other, uq_ref, raw, rows, wq_s, sems):
    head, blocks, _, _ = config
    copies = Copies(sems)
    waits = load_rows(copies, source, place[1], raw, 0, place[0], blocks)
    arrivals = [
        copies.start(weight, wq_s.at[i]) for i, weight in enumerate((wq_own, wq_other))
    ]
    for wait in waits:
        wait.wait()
    normalize_rows(raw, rows, gain)
    for wait in arrivals:
        wait.wait()
    project(rows[...], (wq_s.at[0], wq_s.at[1]), uq_ref, lambda x: unit(x, head))


def memory_kernel(config, place, gain, *refs):
    head, _, _, count = config
    pieces, refs = refs[:count], refs[count:]
    wk_own, wk_other, wv_own, wv_other, uk_ref, v_ref, rows = refs
    normalize_pieces(pieces, rows, gain)
    normed = rows[...]
    project(normed, (wk_own, wk_other), uk_ref, lambda x: unit(x, head))
    project(normed, (wv_own, wv_other), v_ref, lambda x: x.astype(BF16))


def keep_kernel(config, place, *refs):
    count = len(refs) // 2 - 1
    copies = Copies(refs[-1])
    for wait in [copies.start(refs[i], refs[count + i]) for i in range(count)]:
        wait.wait()
    refs[2 * count][...] = jnp.zeros_like(refs[2 * count])


def mix_kernel(config, place, sharp_own, sharp_other, uq, uk, v, wo_own, wo_other, *refs):
    outs, (mixture, own_s, other_s, sems) = refs[:-4], refs[-4:]
    arrivals = stream_out(Copies(sems), ((wo_own, own_s), (wo_other, other_s)))
    attend_all(uq, uk, v, (sharp_own, sharp_other), mixture, config[0])
    project_out(mixture[...], (own_s, other_s), outs, arrivals)


def section_kernel(config, place, sharp_own, sharp_other, gain, *refs):
    head, _, _, count = config
    pieces, refs = refs[:count], refs[count:]
    uk, v, wq_own, wq_other, wo_own, wo_other = refs[:6]
    outs, (rows, uq, mixture) = refs[6:-3], refs[-3:]
    normalize_pieces(pieces, rows, gain)
    project(rows[...], (wq_own, wq_other), uq, lambda x: unit(x, head))
    attend_all(uq, uk, v, (sharp_own, sharp_other), mixture, head)
    project_out(mixture[...], (wo_own, wo_other), outs)


def place_kernel(config, place, *refs):
    _, blocks, _, count = config
    pieces, out = refs[:-1], refs[-1]
    chip, core = place[0], place[1]
    groups = count // blocks
    for i, piece in enumerate(pieces):
        height = piece.shape[0]
        batch = core if i < count else 1 - core
        j, g = (i % count) // groups, i % groups
        at = pl.multiple_of(((chip ^ j) * groups + g) * height, height)
        out[batch, pl.ds(at, height), :] = piece[...]


def shards(
    inbound_embedding_batches,
    decoder_embedding_batches,
    asking_projections,
    probe_projections,
    payload_projections,
    exit_projections,
    layer_rescale_weights,
    logit_sharpness,
    last_rescale_weights,
):
    sections = lax.axis_size("section")
    seq = lax.axis_size("seq")
    section = lax.axis_index("section")
    position = lax.axis_index("seq")
    encoders = 3 * sections // 8
    batches, length, width = inbound_embedding_batches.shape
    cores = 2
    blocks = seq // cores
    assert batches == cores and blocks & (blocks - 1) == 0
    core, chip = position % cores, position // cores
    height = length // blocks
    groups = 2 if height % 32 == 0 else 1
    piece = height // groups
    heads = logit_sharpness.shape[1]
    inner = asking_projections.shape[2]
    head = inner // heads
    both = cores * inner
    count = blocks * groups
    config = (head, blocks, length, count)

    def flip(bits):
        pairs = [(i, i ^ bits) for i in range(seq)]
        return lambda x: lax.ppermute(x, "seq", pairs)

    def up(x, source, target):
        return lax.ppermute(x, "section", [(source, target)])

    to_core = flip(1)
    to_chip = [None] + [flip(j * cores) for j in range(1, blocks)]

    wq, wk, wv, wo = (
        w[0] for w in (asking_projections, probe_projections, payload_projections, exit_projections)
    )
    gain = layer_rescale_weights
    last_gain = last_rescale_weights.reshape(1, width)
    sharp = logit_sharpness[0] * (head ** -0.5)
    sharp_other = to_core(sharp)
    wq_other = to_core(wq)
    stay = pltpu.with_memory_space_constraint

    place = jnp.stack([chip, core, section]).astype(jnp.int32)

    def sds(shape, dtype=BF16):
        return jax.ShapeDtypeStruct(shape, dtype)

    row_scratch = pltpu.VMEM((length, width), BF16)
    out_weight = pltpu.VMEM((inner, width), BF16)
    both_scratch = pltpu.VMEM((length, both), BF16)
    chunks = pltpu.VMEM((inner // WIDE, width, WIDE), BF16)
    partials = [sds((piece, width))] * count

    def sems(n):
        return pltpu.SemaphoreType.DMA((n,))

    def gather(shares):
        by_group = [[share] + [to_chip[j](share) for j in range(1, blocks)] for share in shares]
        return [by_group[g][j] for j in range(blocks) for g in range(groups)]

    def finish(parts, residuals, step):
        shares = []
        for g, residual in enumerate(residuals):
            arrived = [to_chip[j](parts[j * groups + g]) for j in range(1, blocks)]
            shares.append(
                kernel_call(
                    functools.partial(only_in([step])(finish_kernel), config),
                    sds((piece, width)),
                    [IN_SMEM] + [IN_VMEM] * (blocks + 1),
                    [],
                    4,
                )(place, residual, parts[g], *arrived)
            )
        return shares

    def own_rows(source):
        rows = lax.dynamic_slice(source, (core, chip * height, 0), (1, height, width))[0]
        return [rows[g * piece : (g + 1) * piece] for g in range(groups)]

    own, other = kernel_call(
        functools.partial(only_in([0])(first_kernel), config),
        [sds((length, width))] * 2,
        [IN_SMEM, IN_SMEM, IN_VMEM] + [IN_HBM] * 5,
        [pltpu.VMEM((batches * length, width), BF16)] * 2
        + [pltpu.VMEM((width, inner), BF16)] * 3
        + [out_weight]
        + [pltpu.VMEM((batches * length, inner), BF16)] * 4
        + [sems(batches * blocks + 3 + width // OUT_WIDE)],
        32,
    )(place, sharp, gain, *(stay(x, pltpu.HBM) for x in (inbound_embedding_batches, wq, wk, wv, wo)))
    parts = kernel_call(
        functools.partial(only_in([0])(join_kernel), config),
        partials,
        [IN_SMEM] + [IN_VMEM] * 2,
        [],
        8,
    )(place, own, to_core(other))

    unit_queries = kernel_call(
        functools.partial(only_in([encoders])(query_kernel), config),
        sds((length, both)),
        [IN_SMEM, IN_VMEM] + [IN_HBM] * 3,
        [row_scratch, row_scratch, pltpu.VMEM((cores, width, inner), BF16), sems(blocks + cores)],
        18,
        flops=2 * length * width * both,
        moved=2 * width * both,
    )(place, gain, *(stay(x, pltpu.HBM) for x in (decoder_embedding_batches, wq, wq_other)))

    parts, unit_queries, wk, wv = lax.optimization_barrier((parts, unit_queries, wk, wv))
    wk_other, wv_other = to_core(wk), to_core(wv)
    shares = finish(parts, own_rows(inbound_embedding_batches), 0)
    kept = shares
    _, late_wo = lax.optimization_barrier((shares[0], wo))
    wo_other = to_core(late_wo)

    def keep(arrays, users, after):
        after, at_place = lax.optimization_barrier((after, place))
        return kernel_call(
            functools.partial(only_in(users)(keep_kernel), config),
            [pltpu.VMEM(x.shape, x.dtype) for x in arrays] + [sds((8, LANES))],
            [IN_SMEM] + [IN_HBM] * len(arrays),
            [sems(len(arrays))],
            2,
            moved=2 * sum(x.size * x.dtype.itemsize for x in arrays),
        )(at_place, *(stay(x, pltpu.HBM) for x in arrays))

    def project_memory(pieces, scale, users, kv):
        return kernel_call(
            functools.partial(only_in(users)(memory_kernel), config),
            [sds((length, both))] * 2,
            [IN_SMEM] + [IN_VMEM] * (1 + count + 4),
            [row_scratch],
            10,
        )(place, scale, *pieces, *kv)

    queries_and_out = (wq, wq_other, wo, wo_other)
    for step in range(1, sections):
        if step == encoders:
            memory = None
            memory = [up(share, step - 1, step) for share in shares]
            whole, _ = lax.optimization_barrier((jnp.concatenate(shares), memory))
            for target in range(step + 1, sections):
                arrived = up(whole, step - 1, target)
                whole, _ = lax.optimization_barrier((whole, arrived))
                memory = [
                    jnp.where(section == target, arrived[g * piece : (g + 1) * piece], m)
                    for g, m in enumerate(memory)
                ]
            memory, unit_queries = lax.optimization_barrier((memory, unit_queries))
            users = range(step, sections)
            *kv, _ = keep((wk, wk_other, wv, wv_other), users, memory)
            unit_keys, values = project_memory(gather(memory), last_gain, users, kv)
            residuals = own_rows(decoder_embedding_batches)
            parts = kernel_call(
                functools.partial(only_in([step])(mix_kernel), config),
                partials,
                [IN_SMEM] * 3 + [IN_VMEM] * 3 + [IN_HBM] * 2,
                [both_scratch, out_weight, out_weight, sems(2 * (width // OUT_WIDE))],
                16,
            )(
                place, sharp, sharp_other, unit_queries, unit_keys, values,
                stay(wo, pltpu.HBM), stay(wo_other, pltpu.HBM),
            )
            *queries_and_out, mark = keep(
                (wq, wq_other, wo, wo_other), range(step + 1, sections), parts
            )
        else:
            residuals = [up(share, step - 1, step) for share in shares]
            pieces = gather(residuals)
            if step < encoders:
                unit_keys, values = project_memory(pieces, gain, [step], (wk, wk_other, wv, wv_other))
            parts = kernel_call(
                functools.partial(only_in([step])(section_kernel), config),
                partials,
                [IN_SMEM] * 3 + [IN_VMEM] * (1 + count + 6),
                [row_scratch, both_scratch, both_scratch],
                10,
            )(
                place, sharp, sharp_other, gain, *pieces, unit_keys, values,
                *queries_and_out,
            )
        shares = finish(parts, residuals, step)
        if step == encoders:
            shares[-1], _ = lax.optimization_barrier((shares[-1], mark))
        kept = [jnp.where(section == step, share, old) for share, old in zip(shares, kept)]

    pieces = gather(kept)
    pieces = pieces + [to_core(x) for x in pieces]
    finished = kernel_call(
        functools.partial(place_kernel, config),
        sds((batches, length, width)),
        [IN_SMEM] + [IN_VMEM] * len(pieces),
        [],
        8,
    )(place, *pieces)
    return finished[None]


def solution(mesh):
    return jax.shard_map(
        shards,
        mesh=mesh,
        in_specs=(
            P(),
            P(),
            P("section", None, "seq"),
            P("section", None, "seq"),
            P("section", None, "seq"),
            P("section", "seq", None),
            P("section", None),
            P("section", "seq"),
            P(),
        ),
        out_specs=P("section", None, None, None),
        check_vma=False,
    )
```

```python
import functools

import jax
import jax.numpy as jnp
from jax import lax
from jax.experimental import pallas as pl
from jax.experimental.pallas import tpu as pltpu
from jax.sharding import PartitionSpec as P

EPSILON = 1e-06
LANES = 128
WIDE = 256
OUT_WIDE = 1024
STEP = 16
BF16 = jnp.bfloat16
F32 = jnp.float32
MIB = 1024 * 1024
ANY = pl.BlockSpec(memory_space=pl.ANY)
IN_HBM = pl.BlockSpec(memory_space=pltpu.HBM)
IN_VMEM = pl.BlockSpec(memory_space=pltpu.VMEM)
IN_SMEM = pl.BlockSpec(memory_space=pltpu.SMEM)


def kernel_call(body, outs, ins, scratch, vmem, flops=0, moved=0, out_spec=IN_VMEM):
    return pl.pallas_call(
        body,
        out_shape=outs,
        in_specs=ins,
        out_specs=jax.tree.map(lambda _: out_spec, outs),
        scratch_shapes=scratch,
        compiler_params=pltpu.CompilerParams(vmem_limit_bytes=vmem * MIB),
        cost_estimate=pl.CostEstimate(flops=flops, bytes_accessed=moved, transcendentals=0),
    )


class Copies:
    def __init__(self, sems):
        self.sems, self.used = sems, 0

    def start(self, src, dst):
        copy = pltpu.make_async_copy(src, dst, self.sems.at[self.used])
        self.used += 1
        copy.start()
        return copy


def normalize(values, gain):
    values = values.astype(F32)
    factor = lax.rsqrt(jnp.mean(values * values, axis=-1, keepdims=True) + EPSILON)
    return (values * factor * gain).astype(BF16)


def normalize_rows(raw, out, gain):
    def body(i, _):
        at = pl.ds(pl.multiple_of(i * STEP, STEP), STEP)
        out[at, :] = normalize(raw[at, :], gain[...])
        return 0

    lax.fori_loop(0, raw.shape[0] // STEP, body, 0)


def normalize_pieces(pieces, out, gain):
    low = 0
    for piece in pieces:
        height = piece.shape[0]
        out[low : low + height, :] = normalize(piece[...], gain[...])
        low += height


def lane_masks(rows, head):
    lane = lax.broadcasted_iota(jnp.int32, (rows, LANES), 1)
    return [(lane // head) == i for i in range(LANES // head)]


def unit(block, head):
    masks = lane_masks(block.shape[0], head)
    squares = block * block
    factor = None
    for mask in masks:
        total = jnp.sum(jnp.where(mask, squares, 0.0), axis=-1, keepdims=True)
        own = lax.rsqrt(total / head + EPSILON)
        factor = own if factor is None else jnp.where(mask, own, factor)
    return (block * factor).astype(BF16)


def attend(queries, keys, values, scales, head):
    rows = queries.shape[0]
    masks = lane_masks(rows, head)
    stacked = jnp.concatenate(
        [jnp.where(mask, queries, jnp.zeros_like(queries)) for mask in masks], axis=0
    )
    scores = lax.dot_general(
        stacked, keys, (((1,), (1,)), ((), ())), preferred_element_type=F32
    )
    weights = []
    for i, scale in enumerate(scales):
        raised = jnp.exp(scores[i * rows : (i + 1) * rows] * scale)
        weights.append((raised / jnp.sum(raised, axis=-1, keepdims=True)).astype(BF16))
    mixed = jnp.dot(jnp.concatenate(weights, axis=0), values, preferred_element_type=F32)
    out = mixed[:rows]
    for i in range(1, len(scales)):
        out = jnp.where(masks[i], mixed[i * rows : (i + 1) * rows], out)
    return out.astype(BF16)


def attend_all(uq, uk, v, sharps, mixture, head):
    per = LANES // head
    each = sharps[0].shape[0]
    for group in range(uq.shape[1] // LANES):
        lanes = slice(group * LANES, (group + 1) * LANES)
        scales = []
        for i in range(per):
            index = group * per + i
            scales.append(sharps[index // each][index % each])
        mixture[:, lanes] = attend(uq[:, lanes], uk[:, lanes], v[:, lanes], scales, head)


def project(normed, weights, out, finish, wide=WIDE):
    low = 0
    for weight in weights:
        for at in range(0, weight.shape[1], wide):
            product = jnp.dot(normed, weight[:, at : at + wide], preferred_element_type=F32)
            for g in range(0, wide, LANES):
                out[:, low + g : low + g + LANES] = finish(product[:, g : g + LANES])
            low += wide


def project_out(mixture, weights, outs, arrivals=None):
    for at in range(0, weights[0].shape[1], OUT_WIDE):
        for arrival in arrivals[at // OUT_WIDE] if arrivals else ():
            arrival.wait()
        total, low = None, 0
        for weight in weights:
            high = low + weight.shape[0]
            term = jnp.dot(
                mixture[:, low:high], weight[:, at : at + OUT_WIDE], preferred_element_type=F32
            )
            total, low = term if total is None else total + term, high
        total = total.astype(BF16)
        low = 0
        for out in outs:
            out[:, at : at + OUT_WIDE] = total[low : low + out.shape[0]]
            low += out.shape[0]


def load_rows(copies, source, batch, scratch, low, chip, blocks):
    height = source.shape[1] // blocks
    waits = []
    for j in range(blocks):
        at = pl.multiple_of((chip ^ j) * height, height)
        waits.append(
            copies.start(
                source.at[batch, pl.ds(at, height), :],
                scratch.at[pl.ds(low + j * height, height), :],
            )
        )
    return waits


def only_in(sections):
    def wrap(body):
        def wrapped(config, place, *refs):
            here = place[2]
            active = here == sections[0]
            for other in sections[1:]:
                active = active | (here == other)
            pl.when(active)(lambda: body(config, place, *refs))

        return wrapped

    return wrap


def give_rows(raw, outs):
    low = 0
    for out in outs:
        out[...] = raw[low : low + out.shape[0], :]
        low += out.shape[0]


def first_kernel(config, place, sharp, gain, source, wq, wk, wv, wo, own_ref, other_ref, *refs):
    residuals, refs = refs[:-11], refs[-11:]
    raw, rows, wq_s, wk_s, wv_s, wo_s, uq, uk, v, mixture, sems = refs
    head, blocks, length, _ = config
    copies = Copies(sems)
    chip, core = place[0], place[1]
    waits = load_rows(copies, source, core, raw, 0, chip, blocks)
    waits += load_rows(copies, source, 1 - core, raw, length, chip, blocks)
    weights = [copies.start(w, s) for w, s in ((wq, wq_s), (wk, wk_s), (wv, wv_s))]
    arrivals = stream_out(copies, ((wo, wo_s),))
    for wait in waits:
        wait.wait()
    give_rows(raw, residuals)
    normalize_rows(raw, rows, gain)
    normed = rows[...]
    wide = wq.shape[1]
    weights[0].wait()
    project(normed, (wq_s,), uq, lambda x: unit(x, head), wide)
    weights[1].wait()
    project(normed, (wk_s,), uk, lambda x: unit(x, head), wide)
    weights[2].wait()
    project(normed, (wv_s,), v, lambda x: x.astype(BF16), wide)
    for low in (0, length):
        at = pl.ds(low, length)
        attend_all(uq[at, :], uk[at, :], v[at, :], (sharp,), mixture.at[at], head)
    project_out(mixture[...], (wo_s,), (own_ref, other_ref), arrivals)


def join_kernel(config, place, own, other, *outs):
    low = 0
    for out in outs:
        at = pl.ds(low, out.shape[0])
        out[...] = (own[at, :].astype(F32) + other[at, :].astype(F32)).astype(BF16)
        low += out.shape[0]


def finish_kernel(config, place, *refs):
    terms, out = refs[:-1], refs[-1]
    total = terms[0][...].astype(F32)
    for term in terms[1:]:
        total = total + term[...].astype(F32)
    out[...] = total.astype(BF16)


def finish_whole_kernel(config, place, *refs):
    _, blocks, _, count = config
    groups = count // blocks
    residuals, terms, outs = refs[:groups], refs[groups:-groups], refs[-groups:]
    low = 0
    for residual, out in zip(residuals, outs):
        at = pl.ds(low, out.shape[0])
        total = residual[...].astype(F32)
        for term in terms:
            total = total + term[at, :].astype(F32)
        out[...] = total.astype(BF16)
        low += out.shape[0]


def stream_out(copies, pairs):
    arrivals = []
    for at in range(0, pairs[0][0].shape[1], OUT_WIDE):
        columns = pl.ds(at, OUT_WIDE)
        arrivals.append(
            [copies.start(source.at[:, columns], scratch.at[:, columns]) for source, scratch in pairs]
        )
    return arrivals


def query_kernel(config, place, gain, source, wq_own, wq_other, uq_ref, *refs):
    residuals, (raw, rows, wq_s, sems) = refs[:-4], refs[-4:]
    head, blocks, _, _ = config
    copies = Copies(sems)
    waits = load_rows(copies, source, place[1], raw, 0, place[0], blocks)
    arrivals = [
        copies.start(weight, wq_s.at[i]) for i, weight in enumerate((wq_own, wq_other))
    ]
    for wait in waits:
        wait.wait()
    give_rows(raw, residuals)
    normalize_rows(raw, rows, gain)
    for wait in arrivals:
        wait.wait()
    project(rows[...], (wq_s.at[0], wq_s.at[1]), uq_ref, lambda x: unit(x, head))


def memory_kernel(config, place, gain, *refs):
    head = config[0]
    pieces, (wk_own, wk_other, wv_own, wv_other, uk_ref, v_ref, rows) = refs[:-7], refs[-7:]
    normalize_pieces(pieces, rows, gain)
    normed = rows[...]
    project(normed, (wk_own, wk_other), uk_ref, lambda x: unit(x, head))
    project(normed, (wv_own, wv_other), v_ref, lambda x: x.astype(BF16))


def keep_kernel(config, place, *refs):
    sems, refs = refs[-1], refs[:-1]
    count = len(refs) // 2
    copies = Copies(sems)
    for wait in [copies.start(refs[i], refs[count + i]) for i in range(count)]:
        wait.wait()


def keep_keys_kernel(config, place, wk, wv, stack, *refs):
    keep_kernel(config, place, wk, stack.at[0], wv, stack.at[1], *refs)


def stack_kernel(config, place, *refs):
    sources, (out, held, sems) = refs[:-3], refs[-3:]
    copies = Copies(sems)
    arrivals = [copies.start(source, held.at[i]) for i, source in enumerate(sources)]
    leaving = []
    for i, arrival in enumerate(arrivals):
        arrival.wait()
        leaving.append(copies.start(held.at[i], out.at[i]))
    for wait in leaving:
        wait.wait()


def mix_kernel(config, place, sharp_own, sharp_other, uq, uk, v, wo_own, wo_other, *refs):
    outs, (mixture, own_s, other_s, sems) = refs[:-4], refs[-4:]
    arrivals = stream_out(Copies(sems), ((wo_own, own_s), (wo_other, other_s)))
    attend_all(uq, uk, v, (sharp_own, sharp_other), mixture, config[0])
    project_out(mixture[...], (own_s, other_s), outs, arrivals)


def section_kernel(config, place, sharp_own, sharp_other, gain, *refs):
    head, _, _, count = config
    pieces, refs = refs[:count], refs[count:]
    uk, v, wq_own, wq_other, wo_own, wo_other = refs[:6]
    outs, (rows, uq, mixture) = refs[6:-3], refs[-3:]
    normalize_pieces(pieces, rows, gain)
    project(rows[...], (wq_own, wq_other), uq, lambda x: unit(x, head))
    attend_all(uq, uk, v, (sharp_own, sharp_other), mixture, head)
    project_out(mixture[...], (wo_own, wo_other), outs)


def place_kernel(config, place, *refs):
    _, blocks, _, count = config
    pieces, out = refs[:-1], refs[-1]
    chip, core = place[0], place[1]
    groups = count // blocks
    for i, piece in enumerate(pieces):
        height = piece.shape[0]
        batch = core if i < count else 1 - core
        j, g = (i % count) // groups, i % groups
        at = pl.multiple_of(((chip ^ j) * groups + g) * height, height)
        out[batch, pl.ds(at, height), :] = piece[...]


def shards(
    inbound_embedding_batches,
    decoder_embedding_batches,
    asking_projections,
    probe_projections,
    payload_projections,
    exit_projections,
    layer_rescale_weights,
    logit_sharpness,
    last_rescale_weights,
):
    sections = lax.axis_size("section")
    seq = lax.axis_size("seq")
    section = lax.axis_index("section")
    position = lax.axis_index("seq")
    encoders = 3 * sections // 8
    batches, length, width = inbound_embedding_batches.shape
    cores = 2
    blocks = seq // cores
    assert batches == cores and blocks & (blocks - 1) == 0
    core, chip = position % cores, position // cores
    height = length // blocks
    groups = 2 if height % 32 == 0 else 1
    piece = height // groups
    heads = logit_sharpness.shape[1]
    inner = asking_projections.shape[2]
    head = inner // heads
    both = cores * inner
    count = blocks * groups
    config = (head, blocks, length, count)

    def flip(bits):
        pairs = [(i, i ^ bits) for i in range(seq)]
        return lambda x: lax.ppermute(x, "seq", pairs)

    def up(x, source, target):
        return lax.ppermute(x, "section", [(source, target)])

    to_core = flip(1)
    to_chip = [None] + [flip(j * cores) for j in range(1, blocks)]

    wq, wk, wv, wo = (
        w[0] for w in (asking_projections, probe_projections, payload_projections, exit_projections)
    )
    gain = layer_rescale_weights
    last_gain = last_rescale_weights.reshape(1, width)
    sharp = logit_sharpness[0] * (head ** -0.5)
    sharp_other = to_core(sharp)
    wq_other = to_core(wq)
    stay = pltpu.with_memory_space_constraint

    place = jnp.stack([chip, core, section]).astype(jnp.int32)

    def sds(shape, dtype=BF16):
        return jax.ShapeDtypeStruct(shape, dtype)

    row_scratch = pltpu.VMEM((length, width), BF16)
    out_weight = pltpu.VMEM((inner, width), BF16)
    both_scratch = pltpu.VMEM((length, both), BF16)
    chunks = pltpu.VMEM((inner // WIDE, width, WIDE), BF16)
    partials = [sds((piece, width))] * count

    def sems(n):
        return pltpu.SemaphoreType.DMA((n,))

    def gather(shares):
        by_group = [[share] + [to_chip[j](share) for j in range(1, blocks)] for share in shares]
        return [group[j] for j in range(blocks) for group in by_group]

    def finish(parts, residuals, step):
        shares = []
        for g, residual in enumerate(residuals):
            arrived = [to_chip[j](parts[j * groups + g]) for j in range(1, blocks)]
            shares.append(
                kernel_call(
                    functools.partial(only_in([step])(finish_kernel), config),
                    sds((piece, width)),
                    [IN_SMEM] + [IN_VMEM] * (blocks + 1),
                    [],
                    4,
                )(place, residual, parts[g], *arrived)
            )
        return shares

    def finish_whole(parts, residuals, step):
        arrived = [to_chip[j](parts[j]) for j in range(1, blocks)]
        return kernel_call(
            functools.partial(only_in([step])(finish_whole_kernel), config),
            [sds((piece, width))] * groups,
            [IN_SMEM] + [IN_VMEM] * (groups + blocks),
            [],
            6,
        )(place, *residuals, parts[0], *arrived)

    residual_shapes = [sds((piece, width))] * groups
    own, other, *first_residuals = kernel_call(
        functools.partial(only_in([0])(first_kernel), config),
        [sds((length, width))] * 2 + residual_shapes,
        [IN_SMEM, IN_SMEM, IN_VMEM] + [IN_HBM] * 5,
        [pltpu.VMEM((batches * length, width), BF16)] * 2
        + [pltpu.VMEM((width, inner), BF16)] * 3
        + [out_weight]
        + [pltpu.VMEM((batches * length, inner), BF16)] * 4
        + [sems(batches * blocks + 3 + width // OUT_WIDE)],
        32,
    )(place, sharp, gain, *(stay(x, pltpu.HBM) for x in (inbound_embedding_batches, wq, wk, wv, wo)))
    stack = kernel_call(
        functools.partial(only_in(range(1, sections))(stack_kernel), config),
        pltpu.HBM((2, width, inner), BF16),
        [IN_SMEM] + [IN_HBM] * 2,
        [pltpu.VMEM((2, width, inner), BF16), sems(4)],
        10,
        out_spec=IN_HBM,
    )(place, stay(wk, pltpu.HBM), stay(wv, pltpu.HBM))
    received, stack = lax.optimization_barrier((to_core(other), stack))
    parts = kernel_call(
        functools.partial(only_in([0])(join_kernel), config),
        [sds((height, width))] * blocks,
        [IN_SMEM] + [IN_VMEM] * 2,
        [],
        8,
    )(place, own, received)

    unit_queries, *target_residuals = kernel_call(
        functools.partial(only_in([encoders])(query_kernel), config),
        [sds((length, both))] + residual_shapes,
        [IN_SMEM, IN_VMEM] + [IN_HBM] * 3,
        [row_scratch, row_scratch, pltpu.VMEM((cores, width, inner), BF16), sems(blocks + cores)],
        18,
        flops=2 * length * width * both,
        moved=2 * width * both,
    )(place, gain, *(stay(x, pltpu.HBM) for x in (decoder_embedding_batches, wq, wq_other)))

    parts, unit_queries, stack = lax.optimization_barrier((parts, unit_queries, stack))
    stack = to_core(stack)
    shares = finish_whole(parts, first_residuals, 0)
    kept = shares
    _, late_wo = lax.optimization_barrier((shares[0], wo))
    wo_other = to_core(late_wo)

    def keep(body, arrays, shapes, users, after):
        _, at_place = lax.optimization_barrier((after, place))
        return kernel_call(
            functools.partial(only_in(users)(body), config),
            [pltpu.VMEM(shape, BF16) for shape in shapes],
            [IN_SMEM] + [IN_HBM] * len(arrays),
            [sems(4)],
            2,
            moved=8 * width * both,
        )(at_place, *(stay(x, pltpu.HBM) for x in arrays))

    def keep_keys(users, after):
        return keep(keep_keys_kernel, (wk, wv, stack), [(width, inner)] * 4, users, after)

    def keep_queries(users, after):
        arrays = (wq, wq_other, wo, wo_other)
        return keep(keep_kernel, arrays, [x.shape for x in arrays], users, after)

    def project_memory(pieces, scale, users, kv):
        return kernel_call(
            functools.partial(only_in(users)(memory_kernel), config),
            [sds((length, both))] * 2,
            [IN_SMEM] + [IN_VMEM] * (1 + len(pieces) + 4),
            [row_scratch],
            10,
        )(place, scale, *pieces, *kv)

    for step in range(1, sections):
        if step == encoders:
            memory = [up(share, step - 1, step) for share in shares]
            whole, _ = lax.optimization_barrier((jnp.concatenate(shares), memory))
            memory = jnp.concatenate(memory)
            for target in range(step + 1, sections):
                arrived = up(whole, step - 1, target)
                whole, _ = lax.optimization_barrier((whole, arrived))
                memory = jnp.where(section == target, arrived, memory)
            memory, unit_queries = lax.optimization_barrier((memory, unit_queries))
            users = range(step, sections)
            kv = keep_keys(users, memory)
            unit_keys, values = project_memory(gather([memory]), last_gain, users, kv)
            residuals = target_residuals
            parts = kernel_call(
                functools.partial(only_in([step])(mix_kernel), config),
                partials,
                [IN_SMEM] * 3 + [IN_VMEM] * 3 + [IN_HBM] * 2,
                [both_scratch, out_weight, out_weight, sems(2 * (width // OUT_WIDE))],
                16,
            )(
                place, sharp, sharp_other, unit_queries, unit_keys, values,
                stay(wo, pltpu.HBM), stay(wo_other, pltpu.HBM),
            )
        else:
            residuals = [up(share, step - 1, step) for share in shares]
            pieces = gather(residuals)
            if step in (1, encoders + 1):
                queries_and_out = keep_queries(range(step, sections), residuals)
            if step < encoders:
                kv = keep_keys([step], residuals)
                unit_keys, values = project_memory(pieces, gain, [step], kv)
            parts = kernel_call(
                functools.partial(only_in([step])(section_kernel), config),
                partials,
                [IN_SMEM] * 3 + [IN_VMEM] * (1 + count + 6),
                [row_scratch, both_scratch, both_scratch],
                10,
            )(
                place, sharp, sharp_other, gain, *pieces, unit_keys, values,
                *queries_and_out,
            )
        shares = finish(parts, residuals, step)
        kept = [jnp.where(section == step, share, old) for share, old in zip(shares, kept)]

    pieces = gather(kept)
    pieces = pieces + [to_core(x) for x in pieces]
    finished = kernel_call(
        functools.partial(place_kernel, config),
        sds((batches, length, width)),
        [IN_SMEM] + [IN_VMEM] * len(pieces),
        [],
        8,
    )(place, *pieces)
    return finished[None]


def solution(mesh):
    return jax.shard_map(
        shards,
        mesh=mesh,
        in_specs=(
            P(),
            P(),
            P("section", None, "seq"),
            P("section", None, "seq"),
            P("section", None, "seq"),
            P("section", "seq", None),
            P("section", None),
            P("section", "seq"),
            P(),
        ),
        out_specs=P("section", None, None, None),
        check_vma=False,
    )
```

```python
import functools

import jax
import jax.numpy as jnp
from jax import lax
from jax.experimental import pallas as pl
from jax.experimental.pallas import tpu as pltpu
from jax.sharding import PartitionSpec as P

EPSILON = 1e-06
LANES = 128
WIDE = 256
OUT_WIDE = 1024
STEP = 16
BF16 = jnp.bfloat16
F32 = jnp.float32
MIB = 1024 * 1024
ANY = pl.BlockSpec(memory_space=pl.ANY)
IN_HBM = pl.BlockSpec(memory_space=pltpu.HBM)
IN_VMEM = pl.BlockSpec(memory_space=pltpu.VMEM)
IN_SMEM = pl.BlockSpec(memory_space=pltpu.SMEM)


def kernel_call(body, outs, ins, scratch, vmem, flops=0, moved=0):
    return pl.pallas_call(
        body,
        out_shape=outs,
        in_specs=ins,
        out_specs=jax.tree.map(lambda _: IN_VMEM, outs),
        scratch_shapes=scratch,
        compiler_params=pltpu.CompilerParams(vmem_limit_bytes=vmem * MIB),
        cost_estimate=pl.CostEstimate(flops=flops, bytes_accessed=moved, transcendentals=0),
    )


class Copies:
    def __init__(self, sems):
        self.sems, self.used = sems, 0

    def start(self, src, dst):
        copy = pltpu.make_async_copy(src, dst, self.sems.at[self.used])
        self.used += 1
        copy.start()
        return copy


def normalize(values, gain):
    values = values.astype(F32)
    factor = lax.rsqrt(jnp.mean(values * values, axis=-1, keepdims=True) + EPSILON)
    return (values * factor * gain).astype(BF16)


def normalize_rows(raw, out, gain):
    def body(i, _):
        at = pl.ds(pl.multiple_of(i * STEP, STEP), STEP)
        out[at, :] = normalize(raw[at, :], gain[...])
        return 0

    lax.fori_loop(0, raw.shape[0] // STEP, body, 0)


def normalize_pieces(pieces, out, gain):
    low = 0
    for piece in pieces:
        height = piece.shape[0]
        out[low : low + height, :] = normalize(piece[...], gain[...])
        low += height


def lane_masks(rows, head):
    lane = lax.broadcasted_iota(jnp.int32, (rows, LANES), 1)
    return [(lane // head) == i for i in range(LANES // head)]


def unit(block, head):
    masks = lane_masks(block.shape[0], head)
    squares = block * block
    factor = None
    for mask in masks:
        total = jnp.sum(jnp.where(mask, squares, 0.0), axis=-1, keepdims=True)
        own = lax.rsqrt(total / head + EPSILON)
        factor = own if factor is None else jnp.where(mask, own, factor)
    return (block * factor).astype(BF16)


def attend(queries, keys, values, scales, head):
    rows = queries.shape[0]
    masks = lane_masks(rows, head)
    stacked = jnp.concatenate(
        [jnp.where(mask, queries, jnp.zeros_like(queries)) for mask in masks], axis=0
    )
    scores = lax.dot_general(
        stacked, keys, (((1,), (1,)), ((), ())), preferred_element_type=F32
    )
    weights = []
    for i, scale in enumerate(scales):
        raised = jnp.exp(scores[i * rows : (i + 1) * rows] * scale)
        weights.append((raised / jnp.sum(raised, axis=-1, keepdims=True)).astype(BF16))
    mixed = jnp.dot(jnp.concatenate(weights, axis=0), values, preferred_element_type=F32)
    out = mixed[:rows]
    for i in range(1, len(scales)):
        out = jnp.where(masks[i], mixed[i * rows : (i + 1) * rows], out)
    return out.astype(BF16)


def attend_all(uq, uk, v, sharps, mixture, head):
    per = LANES // head
    each = sharps[0].shape[0]
    for group in range(uq.shape[1] // LANES):
        lanes = slice(group * LANES, (group + 1) * LANES)
        scales = []
        for i in range(per):
            index = group * per + i
            scales.append(sharps[index // each][index % each])
        mixture[:, lanes] = attend(uq[:, lanes], uk[:, lanes], v[:, lanes], scales, head)


def project(normed, weights, out, finish, wide=WIDE):
    low = 0
    for weight in weights:
        for at in range(0, weight.shape[1], wide):
            product = jnp.dot(normed, weight[:, at : at + wide], preferred_element_type=F32)
            for g in range(0, wide, LANES):
                out[:, low + g : low + g + LANES] = finish(product[:, g : g + LANES])
            low += wide


def project_out(mixture, weights, outs, arrivals=None):
    for at in range(0, weights[0].shape[1], OUT_WIDE):
        for arrival in arrivals[at // OUT_WIDE] if arrivals else ():
            arrival.wait()
        total, low = None, 0
        for weight in weights:
            high = low + weight.shape[0]
            term = jnp.dot(
                mixture[:, low:high], weight[:, at : at + OUT_WIDE], preferred_element_type=F32
            )
            total, low = term if total is None else total + term, high
        total = total.astype(BF16)
        low = 0
        for out in outs:
            out[:, at : at + OUT_WIDE] = total[low : low + out.shape[0]]
            low += out.shape[0]


def load_rows(copies, source, batch, scratch, low, chip, blocks):
    height = source.shape[1] // blocks
    waits = []
    for j in range(blocks):
        at = pl.multiple_of((chip ^ j) * height, height)
        waits.append(
            copies.start(
                source.at[batch, pl.ds(at, height), :],
                scratch.at[pl.ds(low + j * height, height), :],
            )
        )
    return waits


def only_in(sections):
    def wrap(body):
        def wrapped(config, place, *refs):
            here = place[2]
            active = here == sections[0]
            for other in sections[1:]:
                active = active | (here == other)
            pl.when(active)(lambda: body(config, place, *refs))

        return wrapped

    return wrap


def give_rows(raw, outs):
    low = 0
    for out in outs:
        out[...] = raw[low : low + out.shape[0], :]
        low += out.shape[0]


def first_kernel(config, place, sharp, gain, source, wq, wk, wv, wo, own_ref, other_ref, *refs):
    residuals, refs = refs[:-11], refs[-11:]
    raw, rows, wq_s, wk_s, wv_s, wo_s, uq, uk, v, mixture, sems = refs
    head, blocks, length, _ = config
    copies = Copies(sems)
    chip, core = place[0], place[1]
    waits = load_rows(copies, source, core, raw, 0, chip, blocks)
    waits += load_rows(copies, source, 1 - core, raw, length, chip, blocks)
    weights = [copies.start(w, s) for w, s in ((wq, wq_s), (wk, wk_s), (wv, wv_s))]
    arrivals = stream_out(copies, ((wo, wo_s),))
    for wait in waits:
        wait.wait()
    give_rows(raw, residuals)
    normalize_rows(raw, rows, gain)
    normed = rows[...]
    wide = wq.shape[1]
    weights[0].wait()
    project(normed, (wq_s,), uq, lambda x: unit(x, head), wide)
    weights[1].wait()
    project(normed, (wk_s,), uk, lambda x: unit(x, head), wide)
    weights[2].wait()
    project(normed, (wv_s,), v, lambda x: x.astype(BF16), wide)
    for low in (0, length):
        at = pl.ds(low, length)
        attend_all(uq[at, :], uk[at, :], v[at, :], (sharp,), mixture.at[at], head)
    project_out(mixture[...], (wo_s,), (own_ref, other_ref), arrivals)


def join_kernel(config, place, own, other, *outs):
    low = 0
    for out in outs:
        at = pl.ds(low, out.shape[0])
        out[...] = (own[at, :].astype(F32) + other[at, :].astype(F32)).astype(BF16)
        low += out.shape[0]


def finish_kernel(config, place, *refs):
    terms, out = refs[:-1], refs[-1]
    total = terms[0][...].astype(F32)
    for term in terms[1:]:
        total = total + term[...].astype(F32)
    out[...] = total.astype(BF16)


def stream_out(copies, pairs):
    arrivals = []
    for at in range(0, pairs[0][0].shape[1], OUT_WIDE):
        columns = pl.ds(at, OUT_WIDE)
        arrivals.append(
            [copies.start(source.at[:, columns], scratch.at[:, columns]) for source, scratch in pairs]
        )
    return arrivals


def query_kernel(config, place, gain, source, wq, own_ref, other_ref, *refs):
    residuals, (raw, rows, wq_s, uq, sems) = refs[:-5], refs[-5:]
    head, blocks, length, _ = config
    copies = Copies(sems)
    chip, core = place[0], place[1]
    waits = load_rows(copies, source, core, raw, 0, chip, blocks)
    waits += load_rows(copies, source, 1 - core, raw, length, chip, blocks)
    arrival = copies.start(wq, wq_s)
    for wait in waits:
        wait.wait()
    give_rows(raw, residuals)
    normalize_rows(raw, rows, gain)
    arrival.wait()
    project(rows[...], (wq_s,), uq, lambda x: unit(x, head), wq.shape[1])
    own_ref[...] = uq[:length, :]
    other_ref[...] = uq[length:, :]


def memory_kernel(config, place, gain, *refs):
    head = config[0]
    pieces, (wk_own, wk_other, wv_own, wv_other, uk_ref, v_ref, rows) = refs[:-7], refs[-7:]
    normalize_pieces(pieces, rows, gain)
    normed = rows[...]
    project(normed, (wk_own, wk_other), uk_ref, lambda x: unit(x, head))
    project(normed, (wv_own, wv_other), v_ref, lambda x: x.astype(BF16))


def keep_kernel(config, place, *refs):
    sems, refs = refs[-1], refs[:-1]
    count = len(refs) // 2
    copies = Copies(sems)
    for wait in [copies.start(refs[i], refs[count + i]) for i in range(count)]:
        wait.wait()
    refs[-1][...] = jnp.zeros_like(refs[-1])


def mix_kernel(config, place, sharp_own, sharp_other, uq_own, uq_other, uk, v, *refs):
    wo_own, wo_other, outs, (uq, mixture) = refs[0], refs[1], refs[2:-2], refs[-2:]
    inner = uq_own.shape[1]
    uq[:, :inner] = uq_own[...]
    uq[:, inner:] = uq_other[...]
    attend_all(uq, uk, v, (sharp_own, sharp_other), mixture, config[0])
    project_out(mixture[...], (wo_own, wo_other), outs)


def pass_kernel(share, mark, out):
    out[...] = share[...]


def section_kernel(config, place, sharp_own, sharp_other, gain, *refs):
    head, _, _, count = config
    pieces, refs = refs[:count], refs[count:]
    uk, v, wq_own, wq_other, wo_own, wo_other = refs[:6]
    outs, (rows, uq, mixture) = refs[6:-3], refs[-3:]
    normalize_pieces(pieces, rows, gain)
    project(rows[...], (wq_own, wq_other), uq, lambda x: unit(x, head))
    attend_all(uq, uk, v, (sharp_own, sharp_other), mixture, head)
    project_out(mixture[...], (wo_own, wo_other), outs)


def place_kernel(config, place, *refs):
    _, blocks, _, count = config
    pieces, out = refs[:-1], refs[-1]
    chip, core = place[0], place[1]
    groups = count // blocks
    for i, piece in enumerate(pieces):
        height = piece.shape[0]
        batch = core if i < count else 1 - core
        j, g = (i % count) // groups, i % groups
        at = pl.multiple_of(((chip ^ j) * groups + g) * height, height)
        out[batch, pl.ds(at, height), :] = piece[...]


def shards(
    inbound_embedding_batches,
    decoder_embedding_batches,
    asking_projections,
    probe_projections,
    payload_projections,
    exit_projections,
    layer_rescale_weights,
    logit_sharpness,
    last_rescale_weights,
):
    sections = lax.axis_size("section")
    seq = lax.axis_size("seq")
    section = lax.axis_index("section")
    position = lax.axis_index("seq")
    encoders = 3 * sections // 8
    batches, length, width = inbound_embedding_batches.shape
    cores = 2
    blocks = seq // cores
    assert batches == cores and blocks & (blocks - 1) == 0
    core, chip = position % cores, position // cores
    height = length // blocks
    groups = 2 if height % 32 == 0 else 1
    piece = height // groups
    heads = logit_sharpness.shape[1]
    inner = asking_projections.shape[2]
    head = inner // heads
    both = cores * inner
    count = blocks * groups
    config = (head, blocks, length, count)

    def flip(bits):
        pairs = [(i, i ^ bits) for i in range(seq)]
        return lambda x: lax.ppermute(x, "seq", pairs)

    def up(x, source, target):
        return lax.ppermute(x, "section", [(source, target)])

    to_core = flip(1)
    to_chip = [None] + [flip(j * cores) for j in range(1, blocks)]

    wq, wk, wv, wo = (
        w[0] for w in (asking_projections, probe_projections, payload_projections, exit_projections)
    )
    gain = layer_rescale_weights
    last_gain = last_rescale_weights.reshape(1, width)
    sharp = logit_sharpness[0] * (head ** -0.5)
    sharp_other = to_core(sharp)
    stay = pltpu.with_memory_space_constraint

    place = jnp.stack([chip, core, section]).astype(jnp.int32)

    def sds(shape, dtype=BF16):
        return jax.ShapeDtypeStruct(shape, dtype)

    row_scratch = pltpu.VMEM((length, width), BF16)
    out_weight = pltpu.VMEM((inner, width), BF16)
    both_scratch = pltpu.VMEM((length, both), BF16)
    chunks = pltpu.VMEM((inner // WIDE, width, WIDE), BF16)
    partials = [sds((piece, width))] * count

    def sems(n):
        return pltpu.SemaphoreType.DMA((n,))

    def gather(shares):
        by_group = []
        for share in shares:
            others = {j: to_chip[j](share) for j in reversed(range(1, blocks))}
            by_group.append([share] + [others[j] for j in range(1, blocks)])
        return [group[j] for j in range(blocks) for group in by_group]

    def finish(parts, residuals):
        shares = []
        for g, residual in enumerate(residuals):
            arrived = [to_chip[j](parts[j * groups + g]) for j in reversed(range(1, blocks))]
            shares.append(
                kernel_call(
                    functools.partial(finish_kernel, config),
                    sds((piece, width)),
                    [IN_SMEM] + [IN_VMEM] * (blocks + 1),
                    [],
                    4,
                )(place, residual, parts[g], *arrived)
            )
        return shares

    def finish_whole(parts, residual):
        arrived = [to_chip[j](parts[j]) for j in reversed(range(1, blocks))]
        return kernel_call(
            functools.partial(finish_kernel, config),
            sds((height, width)),
            [IN_SMEM] + [IN_VMEM] * (1 + blocks),
            [],
            6,
        )(place, residual, parts[0], *arrived)

    residual_shapes = [sds((piece, width))] * groups

    def zeros(shapes):
        return [jnp.zeros(x.shape, x.dtype) for x in shapes]

    def choose(chosen, body, shapes):
        return lax.cond(chosen, lambda: list(body()), lambda: zeros(shapes))

    def first_section():
        own, other, residual = kernel_call(
            functools.partial(first_kernel, config),
            [sds((length, width))] * 2 + [sds((height, width))],
            [IN_SMEM, IN_SMEM, IN_VMEM] + [IN_HBM] * 5,
            [pltpu.VMEM((batches * length, width), BF16)] * 2
            + [pltpu.VMEM((width, inner), BF16)] * 3
            + [out_weight]
            + [pltpu.VMEM((batches * length, inner), BF16)] * 4
            + [sems(batches * blocks + 3 + width // OUT_WIDE)],
            32,
        )(
            place, sharp, gain,
            *(stay(x, pltpu.HBM) for x in (inbound_embedding_batches, wq, wk, wv, wo)),
        )
        parts = kernel_call(
            functools.partial(join_kernel, config),
            [sds((height, width))] * blocks,
            [IN_SMEM] + [IN_VMEM] * 2,
            [],
            8,
        )(place, own, to_core(other))
        return [finish_whole(parts, residual)]

    def decoder_queries():
        own, other, *residuals = kernel_call(
            functools.partial(query_kernel, config),
            [sds((length, inner))] * 2 + residual_shapes,
            [IN_SMEM, IN_VMEM] + [IN_HBM] * 2,
            [pltpu.VMEM((batches * length, width), BF16)] * 2
            + [pltpu.VMEM((width, inner), BF16), pltpu.VMEM((batches * length, inner), BF16)]
            + [sems(batches * blocks + 1)],
            20,
        )(place, gain, *(stay(x, pltpu.HBM) for x in (decoder_embedding_batches, wq)))
        return [own, to_core(other), *residuals]

    def exchange():
        return [to_core(w) for w in (wk, wv, wo, wq)]

    def no_exchange():
        arrays = [wk, wv, wo, wq] + query_shapes
        return list(
            pl.pallas_call(
                lambda *refs: None,
                out_shape=[pltpu.HBM(x.shape, x.dtype) for x in arrays],
                out_specs=[IN_HBM] * len(arrays),
            )()
        )

    share_shape = [sds((height, width))]
    query_shapes = [sds((length, inner))] * 2 + residual_shapes
    whole, wk_other, wv_other, wo_other, wq_other, queries_own, queries_other, *target_residuals = lax.switch(
        jnp.where(section == 0, 0, jnp.where(section == encoders, 1, 2)),
        [
            lambda: first_section() + no_exchange(),
            lambda: zeros(share_shape) + exchange() + decoder_queries(),
            lambda: zeros(share_shape) + exchange() + zeros(query_shapes),
        ],
    )
    kept = whole

    def keep(arrays, after, users=None):
        _, at_place = lax.optimization_barrier((after, place))
        body = keep_kernel if users is None else only_in(users)(keep_kernel)
        return kernel_call(
            functools.partial(body, config),
            [pltpu.VMEM(x.shape, BF16) for x in arrays] + [sds((8, LANES))],
            [IN_SMEM] + [IN_HBM] * len(arrays),
            [sems(len(arrays))],
            2,
            moved=4 * len(arrays) * width * inner,
        )(at_place, *(stay(x, pltpu.HBM) for x in arrays))

    def project_memory(pieces, scale, kv):
        return kernel_call(
            functools.partial(memory_kernel, config),
            [sds((length, both))] * 2,
            [IN_SMEM] + [IN_VMEM] * (1 + len(pieces) + 4),
            [row_scratch],
            10,
        )(place, scale, *pieces, *kv)

    def first_decoder(memory):
        *near, _ = keep((wk, wk_other, wv, wv_other, wo, wo_other), memory)
        keys_values = list(project_memory(gather([memory]), last_gain, near[:4]))
        parts = kernel_call(
            functools.partial(mix_kernel, config),
            partials,
            [IN_SMEM] * 3 + [IN_VMEM] * 6,
            [both_scratch, both_scratch],
            12,
        )(place, sharp, sharp_other, queries_own, queries_other, *keys_values, *near[4:])
        return keys_values + finish(parts, target_residuals)

    def other_sections(share):
        arrived = {target: up(share, encoders - 1, target) for target in range(encoders + 1, sections)}
        memory = arrived[sections - 1]
        for target in reversed(range(encoders + 1, sections - 1)):
            memory = jnp.where(section == target, arrived[target], memory)
        *near, _ = keep((wk, wk_other, wv, wv_other), memory)
        keys_values = list(project_memory(gather([memory]), last_gain, near))
        return keys_values + zeros(residual_shapes)

    def halves(share):
        return [share[g * piece : (g + 1) * piece] for g in range(groups)]

    kept = halves(kept)
    shares = kept
    unit_keys = whole
    for step in range(1, sections):
        if step == encoders:
            if step > 1:
                whole = jnp.concatenate(shares)
            memory = up(whole, step - 1, step)
            unit_keys, values, *shares = lax.cond(
                section == step,
                functools.partial(first_decoder, memory),
                functools.partial(other_sections, whole),
            )
        else:
            if step in (1, encoders + 1):
                *near, mark = keep((wq, wq_other, wo, wo_other), unit_keys, range(step, sections))
                shares[-1] = kernel_call(
                    pass_kernel, sds((piece, width)), [IN_VMEM] * 2, [], 4
                )(shares[-1], mark)
            residuals = [up(share, step - 1, step) for share in shares]
            pieces = gather(residuals)
            if step < encoders:
                *kv, _ = keep((wk, wk_other, wv, wv_other), residuals)
                unit_keys, values = project_memory(pieces, gain, kv)
            parts = kernel_call(
                functools.partial(only_in([step])(section_kernel), config),
                partials,
                [IN_SMEM] * 3 + [IN_VMEM] * (1 + count + 6),
                [row_scratch, both_scratch, both_scratch],
                10,
            )(place, sharp, sharp_other, gain, *pieces, unit_keys, values, *near)
            shares = finish(parts, residuals)
        kept = [jnp.where(section == step, share, old) for share, old in zip(shares, kept)]

    pieces = gather(kept)
    pieces = pieces + [to_core(x) for x in pieces]
    finished = kernel_call(
        functools.partial(place_kernel, config),
        sds((batches, length, width)),
        [IN_SMEM] + [IN_VMEM] * len(pieces),
        [],
        8,
    )(place, *pieces)
    return finished[None]


def solution(mesh):
    return jax.shard_map(
        shards,
        mesh=mesh,
        in_specs=(
            P(),
            P(),
            P("section", None, "seq"),
            P("section", None, "seq"),
            P("section", None, "seq"),
            P("section", "seq", None),
            P("section", None),
            P("section", "seq"),
            P(),
        ),
        out_specs=P("section", None, None, None),
        check_vma=False,
    )
```

```python
import functools

import jax
import jax.numpy as jnp
from jax import lax
from jax.experimental import pallas as pl
from jax.experimental.pallas import tpu as pltpu
from jax.sharding import PartitionSpec as P

EPSILON = 1e-06
LANES = 128
WIDE = 256
OUT_WIDE = 1024
STEP = 16
BF16 = jnp.bfloat16
F32 = jnp.float32
MIB = 1024 * 1024
ANY = pl.BlockSpec(memory_space=pl.ANY)
IN_HBM = pl.BlockSpec(memory_space=pltpu.HBM)
IN_VMEM = pl.BlockSpec(memory_space=pltpu.VMEM)
IN_SMEM = pl.BlockSpec(memory_space=pltpu.SMEM)


def kernel_call(body, outs, ins, scratch, vmem, flops=0, moved=0):
    return pl.pallas_call(
        body,
        out_shape=outs,
        in_specs=ins,
        out_specs=jax.tree.map(lambda _: IN_VMEM, outs),
        scratch_shapes=scratch,
        compiler_params=pltpu.CompilerParams(vmem_limit_bytes=vmem * MIB),
        cost_estimate=pl.CostEstimate(flops=flops, bytes_accessed=moved, transcendentals=0),
    )


class Copies:
    def __init__(self, sems):
        self.sems, self.used = sems, 0

    def start(self, src, dst):
        copy = pltpu.make_async_copy(src, dst, self.sems.at[self.used])
        self.used += 1
        copy.start()
        return copy


def normalize(values, gain):
    values = values.astype(F32)
    factor = lax.rsqrt(jnp.mean(values * values, axis=-1, keepdims=True) + EPSILON)
    return (values * factor * gain).astype(BF16)


def normalize_rows(raw, out, gain):
    def body(i, _):
        at = pl.ds(pl.multiple_of(i * STEP, STEP), STEP)
        out[at, :] = normalize(raw[at, :], gain[...])
        return 0

    lax.fori_loop(0, raw.shape[0] // STEP, body, 0)


def normalize_pieces(pieces, out, gain):
    low = 0
    for piece in pieces:
        height = piece.shape[0]
        out[low : low + height, :] = normalize(piece[...], gain[...])
        low += height


def lane_masks(rows, head):
    lane = lax.broadcasted_iota(jnp.int32, (rows, LANES), 1)
    return [(lane // head) == i for i in range(LANES // head)]


def unit(block, head):
    masks = lane_masks(block.shape[0], head)
    squares = block * block
    factor = None
    for mask in masks:
        total = jnp.sum(jnp.where(mask, squares, 0.0), axis=-1, keepdims=True)
        own = lax.rsqrt(total / head + EPSILON)
        factor = own if factor is None else jnp.where(mask, own, factor)
    return (block * factor).astype(BF16)


def attend(queries, keys, values, scales, head):
    rows = queries.shape[0]
    masks = lane_masks(rows, head)
    stacked = jnp.concatenate(
        [jnp.where(mask, queries, jnp.zeros_like(queries)) for mask in masks], axis=0
    )
    scores = lax.dot_general(
        stacked, keys, (((1,), (1,)), ((), ())), preferred_element_type=F32
    )
    weights = []
    for i, scale in enumerate(scales):
        raised = jnp.exp(scores[i * rows : (i + 1) * rows] * scale)
        weights.append((raised / jnp.sum(raised, axis=-1, keepdims=True)).astype(BF16))
    mixed = jnp.dot(jnp.concatenate(weights, axis=0), values, preferred_element_type=F32)
    out = mixed[:rows]
    for i in range(1, len(scales)):
        out = jnp.where(masks[i], mixed[i * rows : (i + 1) * rows], out)
    return out.astype(BF16)


def attend_all(uq, uk, v, sharps, mixture, head):
    per = LANES // head
    each = sharps[0].shape[0]
    for group in range(uq.shape[1] // LANES):
        lanes = slice(group * LANES, (group + 1) * LANES)
        scales = []
        for i in range(per):
            index = group * per + i
            scales.append(sharps[index // each][index % each] * (head ** -0.5))
        mixture[:, lanes] = attend(uq[:, lanes], uk[:, lanes], v[:, lanes], scales, head)


def project(normed, weights, out, finish, wide=WIDE):
    low = 0
    for weight in weights:
        for at in range(0, weight.shape[1], wide):
            product = jnp.dot(normed, weight[:, at : at + wide], preferred_element_type=F32)
            for g in range(0, wide, LANES):
                out[:, low + g : low + g + LANES] = finish(product[:, g : g + LANES])
            low += wide


def project_out(mixture, weights, outs, arrivals=None):
    for at in range(0, weights[0].shape[1], OUT_WIDE):
        for arrival in arrivals[at // OUT_WIDE] if arrivals else ():
            arrival.wait()
        total, low = None, 0
        for weight in weights:
            high = low + weight.shape[0]
            term = jnp.dot(
                mixture[:, low:high], weight[:, at : at + OUT_WIDE], preferred_element_type=F32
            )
            total, low = term if total is None else total + term, high
        total = total.astype(BF16)
        low = 0
        for out in outs:
            out[:, at : at + OUT_WIDE] = total[low : low + out.shape[0]]
            low += out.shape[0]


def load_rows(copies, source, batch, scratch, low, chip, blocks):
    height = source.shape[1] // blocks
    waits = []
    for j in range(blocks):
        at = pl.multiple_of((chip ^ j) * height, height)
        waits.append(
            copies.start(
                source.at[batch, pl.ds(at, height), :],
                scratch.at[pl.ds(low + j * height, height), :],
            )
        )
    return waits


def only_in(sections):
    def wrap(body):
        def wrapped(config, place, *refs):
            here = place[2]
            active = here == sections[0]
            for other in sections[1:]:
                active = active | (here == other)
            pl.when(active)(lambda: body(config, place, *refs))

        return wrapped

    return wrap


def give_rows(raw, outs):
    low = 0
    for out in outs:
        out[...] = raw[low : low + out.shape[0], :]
        low += out.shape[0]


def first_kernel(config, place, sharp, gain, source, wq, wk, wv, wo, own_ref, other_ref, *refs):
    residuals, refs = refs[:-11], refs[-11:]
    raw, rows, wq_s, wk_s, wv_s, wo_s, uq, uk, v, mixture, sems = refs
    head, blocks, length, _ = config
    copies = Copies(sems)
    chip, core = place[0], place[1]
    waits = load_rows(copies, source, core, raw, 0, chip, blocks)
    waits += load_rows(copies, source, 1 - core, raw, length, chip, blocks)
    weights = [copies.start(w, s) for w, s in ((wq, wq_s), (wk, wk_s), (wv, wv_s))]
    arrivals = stream_out(copies, ((wo, wo_s),))
    for wait in waits:
        wait.wait()
    give_rows(raw, residuals)
    normalize_rows(raw, rows, gain)
    normed = rows[...]
    wide = wq.shape[1]
    weights[0].wait()
    project(normed, (wq_s,), uq, lambda x: unit(x, head), wide)
    weights[1].wait()
    project(normed, (wk_s,), uk, lambda x: unit(x, head), wide)
    weights[2].wait()
    project(normed, (wv_s,), v, lambda x: x.astype(BF16), wide)
    for low in (0, length):
        at = pl.ds(low, length)
        attend_all(uq[at, :], uk[at, :], v[at, :], (sharp,), mixture.at[at], head)
    project_out(mixture[...], (wo_s,), (own_ref, other_ref), arrivals)


def join_kernel(config, place, own, other, *outs):
    low = 0
    for out in outs:
        at = pl.ds(low, out.shape[0])
        out[...] = (own[at, :].astype(F32) + other[at, :].astype(F32)).astype(BF16)
        low += out.shape[0]


def finish_kernel(config, place, *refs):
    terms, out = refs[:-1], refs[-1]
    total = terms[0][...].astype(F32)
    for term in terms[1:]:
        total = total + term[...].astype(F32)
    out[...] = total.astype(BF16)


def stream_out(copies, pairs):
    arrivals = []
    for at in range(0, pairs[0][0].shape[1], OUT_WIDE):
        columns = pl.ds(at, OUT_WIDE)
        arrivals.append(
            [copies.start(source.at[:, columns], scratch.at[:, columns]) for source, scratch in pairs]
        )
    return arrivals


def query_kernel(config, place, gain, source, wq, own_ref, other_ref, *refs):
    residuals, (raw, rows, wq_s, uq, sems) = refs[:-5], refs[-5:]
    head, blocks, length, _ = config
    copies = Copies(sems)
    chip, core = place[0], place[1]
    waits = load_rows(copies, source, core, raw, 0, chip, blocks)
    waits += load_rows(copies, source, 1 - core, raw, length, chip, blocks)
    arrival = copies.start(wq, wq_s)
    for wait in waits:
        wait.wait()
    give_rows(raw, residuals)
    normalize_rows(raw, rows, gain)
    arrival.wait()
    project(rows[...], (wq_s,), uq, lambda x: unit(x, head), wq.shape[1])
    own_ref[...] = uq[:length, :]
    other_ref[...] = uq[length:, :]


def memory_kernel(config, place, gain, *refs):
    head = config[0]
    pieces, (wk_own, wk_other, wv_own, wv_other, uk_ref, v_ref, rows) = refs[:-7], refs[-7:]
    normalize_pieces(pieces, rows, gain)
    normed = rows[...]
    project(normed, (wk_own, wk_other), uk_ref, lambda x: unit(x, head))
    project(normed, (wv_own, wv_other), v_ref, lambda x: x.astype(BF16))


def keep_kernel(config, place, *refs):
    sems, refs = refs[-1], refs[:-1]
    count = len(refs) // 2
    copies = Copies(sems)
    for wait in [copies.start(refs[i], refs[count + i]) for i in range(count)]:
        wait.wait()
    refs[-1][...] = jnp.zeros_like(refs[-1])


def mix_kernel(config, place, sharp_own, sharp_other, uq_own, uq_other, uk, v, *refs):
    wo_own, wo_other, outs, (uq, mixture) = refs[0], refs[1], refs[2:-2], refs[-2:]
    inner = uq_own.shape[1]
    uq[:, :inner] = uq_own[...]
    uq[:, inner:] = uq_other[...]
    attend_all(uq, uk, v, (sharp_own, sharp_other), mixture, config[0])
    project_out(mixture[...], (wo_own, wo_other), outs)


def pass_kernel(share, mark, out):
    out[...] = share[...]


def section_kernel(config, place, sharp_own, sharp_other, gain, *refs):
    head, _, _, count = config
    pieces, refs = refs[:count], refs[count:]
    uk, v, wq_own, wq_other, wo_own, wo_other = refs[:6]
    outs, (rows, uq, mixture) = refs[6:-3], refs[-3:]
    normalize_pieces(pieces, rows, gain)
    project(rows[...], (wq_own, wq_other), uq, lambda x: unit(x, head))
    attend_all(uq, uk, v, (sharp_own, sharp_other), mixture, head)
    project_out(mixture[...], (wo_own, wo_other), outs)


def place_kernel(config, place, *refs):
    _, blocks, _, count = config
    pieces, out = refs[:-1], refs[-1]
    chip, core = place[0], place[1]
    groups = count // blocks
    for i, piece in enumerate(pieces):
        height = piece.shape[0]
        batch = core if i < count else 1 - core
        j, g = (i % count) // groups, i % groups
        at = pl.multiple_of(((chip ^ j) * groups + g) * height, height)
        out[batch, pl.ds(at, height), :] = piece[...]


def shards(
    inbound_embedding_batches,
    decoder_embedding_batches,
    asking_projections,
    probe_projections,
    payload_projections,
    exit_projections,
    layer_rescale_weights,
    logit_sharpness,
    last_rescale_weights,
):
    sections = lax.axis_size("section")
    seq = lax.axis_size("seq")
    section = lax.axis_index("section")
    position = lax.axis_index("seq")
    encoders = 3 * sections // 8
    batches, length, width = inbound_embedding_batches.shape
    cores = 2
    blocks = seq // cores
    assert batches == cores and blocks & (blocks - 1) == 0
    core, chip = position % cores, position // cores
    height = length // blocks
    groups = 2 if height % 32 == 0 else 1
    piece = height // groups
    heads = logit_sharpness.shape[1]
    inner = asking_projections.shape[2]
    head = inner // heads
    both = cores * inner
    count = blocks * groups
    config = (head, blocks, length, count)

    def flip(bits):
        pairs = [(i, i ^ bits) for i in range(seq)]
        return lambda x: lax.ppermute(x, "seq", pairs)

    def up(x, source, target):
        return lax.ppermute(x, "section", [(source, target)])

    to_core = flip(1)
    to_chip = [None] + [flip(j * cores) for j in range(1, blocks)]

    wq, wk, wv, wo = (
        w[0] for w in (asking_projections, probe_projections, payload_projections, exit_projections)
    )
    gain = layer_rescale_weights
    last_gain = last_rescale_weights.reshape(1, width)
    sharp = logit_sharpness[0]
    sharp_other = to_core(sharp)
    stay = pltpu.with_memory_space_constraint

    place = jnp.stack([chip, core, section]).astype(jnp.int32)

    def sds(shape, dtype=BF16):
        return jax.ShapeDtypeStruct(shape, dtype)

    row_scratch = pltpu.VMEM((length, width), BF16)
    out_weight = pltpu.VMEM((inner, width), BF16)
    both_scratch = pltpu.VMEM((length, both), BF16)
    chunks = pltpu.VMEM((inner // WIDE, width, WIDE), BF16)
    partials = [sds((piece, width))] * count

    def sems(n):
        return pltpu.SemaphoreType.DMA((n,))

    def gather(shares):
        if blocks == 4 and len(shares) == 2:
            first, second = shares
            x_first, y_second = to_chip[1](first), to_chip[2](second)
            y_first, x_second = to_chip[2](first), to_chip[1](second)
            by_group = [
                [first, x_first, y_first, to_chip[2](x_first)],
                [second, x_second, y_second, to_chip[1](y_second)],
            ]
        else:
            by_group = []
            for share in shares:
                others = {j: to_chip[j](share) for j in reversed(range(1, blocks))}
                by_group.append([share] + [others[j] for j in range(1, blocks)])
        return [group[j] for j in range(blocks) for group in by_group]

    def finish(parts, residuals):
        shares = []
        for g, residual in enumerate(residuals):
            arrived = [to_chip[j](parts[j * groups + g]) for j in reversed(range(1, blocks))]
            shares.append(
                kernel_call(
                    functools.partial(finish_kernel, config),
                    sds((piece, width)),
                    [IN_SMEM] + [IN_VMEM] * (blocks + 1),
                    [],
                    4,
                )(place, residual, parts[g], *arrived)
            )
        return shares

    def finish_whole(parts, residual):
        arrived = [to_chip[j](parts[j]) for j in reversed(range(1, blocks))]
        return kernel_call(
            functools.partial(finish_kernel, config),
            sds((height, width)),
            [IN_SMEM] + [IN_VMEM] * (1 + blocks),
            [],
            6,
        )(place, residual, parts[0], *arrived)

    residual_shapes = [sds((piece, width))] * groups

    def zeros(shapes):
        return [jnp.zeros(x.shape, x.dtype) for x in shapes]

    def choose(chosen, body, shapes):
        return lax.cond(chosen, lambda: list(body()), lambda: zeros(shapes))

    def first_section():
        own, other, residual = kernel_call(
            functools.partial(first_kernel, config),
            [sds((length, width))] * 2 + [sds((height, width))],
            [IN_SMEM, IN_SMEM, IN_VMEM] + [IN_HBM] * 5,
            [pltpu.VMEM((batches * length, width), BF16)] * 2
            + [pltpu.VMEM((width, inner), BF16)] * 3
            + [out_weight]
            + [pltpu.VMEM((batches * length, inner), BF16)] * 4
            + [sems(batches * blocks + 3 + width // OUT_WIDE)],
            32,
        )(
            place, sharp, gain,
            *(stay(x, pltpu.HBM) for x in (inbound_embedding_batches, wq, wk, wv, wo)),
        )
        parts = kernel_call(
            functools.partial(join_kernel, config),
            [sds((height, width))] * blocks,
            [IN_SMEM] + [IN_VMEM] * 2,
            [],
            8,
        )(place, own, to_core(other))
        return [finish_whole(parts, residual)]

    def decoder_queries():
        own, other, *residuals = kernel_call(
            functools.partial(query_kernel, config),
            [sds((length, inner))] * 2 + residual_shapes,
            [IN_SMEM, IN_VMEM] + [IN_HBM] * 2,
            [pltpu.VMEM((batches * length, width), BF16)] * 2
            + [pltpu.VMEM((width, inner), BF16), pltpu.VMEM((batches * length, inner), BF16)]
            + [sems(batches * blocks + 1)],
            20,
        )(place, gain, *(stay(x, pltpu.HBM) for x in (decoder_embedding_batches, wq)))
        return [own, to_core(other), *residuals]

    def exchange():
        return [to_core(w) for w in (wk, wv, wo, wq)]

    def no_exchange():
        arrays = [wk, wv, wo, wq] + query_shapes
        return list(
            pl.pallas_call(
                lambda *refs: None,
                out_shape=[pltpu.HBM(x.shape, x.dtype) for x in arrays],
                out_specs=[IN_HBM] * len(arrays),
            )()
        )

    share_shape = [sds((height, width))]
    query_shapes = [sds((length, inner))] * 2 + residual_shapes
    whole, wk_other, wv_other, wo_other, wq_other, queries_own, queries_other, *target_residuals = lax.switch(
        jnp.where(section == 0, 0, jnp.where(section == encoders, 1, 2)),
        [
            lambda: first_section() + no_exchange(),
            lambda: zeros(share_shape) + exchange() + decoder_queries(),
            lambda: zeros(share_shape) + exchange() + zeros(query_shapes),
        ],
    )
    kept = whole

    def keep(arrays, after, users=None):
        _, at_place = lax.optimization_barrier((after, place))
        body = keep_kernel if users is None else only_in(users)(keep_kernel)
        return kernel_call(
            functools.partial(body, config),
            [pltpu.VMEM(x.shape, BF16) for x in arrays] + [sds((8, LANES))],
            [IN_SMEM] + [IN_HBM] * len(arrays),
            [sems(len(arrays))],
            2,
            moved=4 * len(arrays) * width * inner,
        )(at_place, *(stay(x, pltpu.HBM) for x in arrays))

    def project_memory(pieces, scale, kv):
        return kernel_call(
            functools.partial(memory_kernel, config),
            [sds((length, both))] * 2,
            [IN_SMEM] + [IN_VMEM] * (1 + len(pieces) + 4),
            [row_scratch],
            10,
        )(place, scale, *pieces, *kv)

    def first_decoder(memory):
        *near, _ = keep((wk, wk_other, wv, wv_other, wo, wo_other), memory)
        keys_values = list(project_memory(gather([memory]), last_gain, near[:4]))
        parts = kernel_call(
            functools.partial(mix_kernel, config),
            partials,
            [IN_SMEM] * 3 + [IN_VMEM] * 6,
            [both_scratch, both_scratch],
            12,
        )(place, sharp, sharp_other, queries_own, queries_other, *keys_values, *near[4:])
        return keys_values + finish(parts, target_residuals)

    def other_sections(share):
        arrived = {target: up(share, encoders - 1, target) for target in range(encoders + 1, sections)}
        memory = arrived[sections - 1]
        for target in reversed(range(encoders + 1, sections - 1)):
            memory = jnp.where(section == target, arrived[target], memory)
        *near, _ = keep((wk, wk_other, wv, wv_other), memory)
        keys_values = list(project_memory(gather([memory]), last_gain, near))
        return keys_values + zeros(residual_shapes)

    def halves(share):
        return [share[g * piece : (g + 1) * piece] for g in range(groups)]

    kept = halves(kept)
    shares = kept
    unit_keys = whole
    for step in range(1, sections):
        if step == encoders:
            if step > 1:
                whole = jnp.concatenate(shares)
            memory = up(whole, step - 1, step)
            unit_keys, values, *shares = lax.cond(
                section == step,
                functools.partial(first_decoder, memory),
                functools.partial(other_sections, whole),
            )
        else:
            if step in (1, encoders + 1):
                *near, mark = keep((wq, wq_other, wo, wo_other), unit_keys, range(step, sections))
                shares[-1] = kernel_call(
                    pass_kernel, sds((piece, width)), [IN_VMEM] * 2, [], 4
                )(shares[-1], mark)
            residuals = [up(share, step - 1, step) for share in shares]
            pieces = gather(residuals)
            if step < encoders:
                *kv, _ = keep((wk, wk_other, wv, wv_other), residuals)
                unit_keys, values = project_memory(pieces, gain, kv)
            parts = kernel_call(
                functools.partial(only_in([step])(section_kernel), config),
                partials,
                [IN_SMEM] * 3 + [IN_VMEM] * (1 + count + 6),
                [row_scratch, both_scratch, both_scratch],
                10,
            )(place, sharp, sharp_other, gain, *pieces, unit_keys, values, *near)
            shares = finish(parts, residuals)
        kept = [jnp.where(section == step, share, old) for share, old in zip(shares, kept)]

    pieces = gather(kept)
    pieces = pieces + [to_core(x) for x in pieces]
    finished = kernel_call(
        functools.partial(place_kernel, config),
        sds((batches, length, width)),
        [IN_SMEM] + [IN_VMEM] * len(pieces),
        [],
        8,
    )(place, *pieces)
    return finished[None]


def solution(mesh):
    return jax.shard_map(
        shards,
        mesh=mesh,
        in_specs=(
            P(),
            P(),
            P("section", None, "seq"),
            P("section", None, "seq"),
            P("section", None, "seq"),
            P("section", "seq", None),
            P("section", None),
            P("section", "seq"),
            P(),
        ),
        out_specs=P("section", None, None, None),
        check_vma=False,
    )
```

```python
import functools

import jax
import jax.numpy as jnp
from jax import lax
from jax.experimental import pallas as pl
from jax.experimental.pallas import tpu as pltpu
from jax.sharding import PartitionSpec as P

EPSILON = 1e-06
LANES = 128
WIDE = 256
OUT_WIDE = 1024
STEP = 16
BF16 = jnp.bfloat16
F32 = jnp.float32
MIB = 1024 * 1024
ANY = pl.BlockSpec(memory_space=pl.ANY)
IN_HBM = pl.BlockSpec(memory_space=pltpu.HBM)
IN_VMEM = pl.BlockSpec(memory_space=pltpu.VMEM)
IN_SMEM = pl.BlockSpec(memory_space=pltpu.SMEM)


def kernel_call(body, outs, ins, scratch, vmem, flops=0, moved=0):
    return pl.pallas_call(
        body,
        out_shape=outs,
        in_specs=ins,
        out_specs=jax.tree.map(lambda _: IN_VMEM, outs),
        scratch_shapes=scratch,
        compiler_params=pltpu.CompilerParams(vmem_limit_bytes=vmem * MIB),
        cost_estimate=pl.CostEstimate(flops=flops, bytes_accessed=moved, transcendentals=0),
    )


class Copies:
    def __init__(self, sems):
        self.sems, self.used = sems, 0

    def start(self, src, dst):
        copy = pltpu.make_async_copy(src, dst, self.sems.at[self.used])
        self.used += 1
        copy.start()
        return copy


def normalize(values, gain):
    values = values.astype(F32)
    factor = lax.rsqrt(jnp.mean(values * values, axis=-1, keepdims=True) + EPSILON)
    return (values * factor * gain).astype(BF16)


def normalize_rows(raw, out, gain):
    def body(i, _):
        at = pl.ds(pl.multiple_of(i * STEP, STEP), STEP)
        out[at, :] = normalize(raw[at, :], gain[...])
        return 0

    lax.fori_loop(0, raw.shape[0] // STEP, body, 0)


def normalize_pieces(pieces, out, gain):
    low = 0
    for piece in pieces:
        height = piece.shape[0]
        out[low : low + height, :] = normalize(piece[...], gain[...])
        low += height


def lane_masks(rows, head):
    lane = lax.broadcasted_iota(jnp.int32, (rows, LANES), 1)
    return [(lane // head) == i for i in range(LANES // head)]


def unit(block, head):
    masks = lane_masks(block.shape[0], head)
    squares = block * block
    factor = None
    for mask in masks:
        total = jnp.sum(jnp.where(mask, squares, 0.0), axis=-1, keepdims=True)
        own = lax.rsqrt(total / head + EPSILON)
        factor = own if factor is None else jnp.where(mask, own, factor)
    return (block * factor).astype(BF16)


def attend(queries, keys, values, scales, head):
    rows = queries.shape[0]
    masks = lane_masks(rows, head)
    stacked = jnp.concatenate(
        [jnp.where(mask, queries, jnp.zeros_like(queries)) for mask in masks], axis=0
    )
    scores = lax.dot_general(
        stacked, keys, (((1,), (1,)), ((), ())), preferred_element_type=F32
    )
    weights = []
    for i, scale in enumerate(scales):
        raised = jnp.exp(scores[i * rows : (i + 1) * rows] * scale)
        weights.append((raised / jnp.sum(raised, axis=-1, keepdims=True)).astype(BF16))
    mixed = jnp.dot(jnp.concatenate(weights, axis=0), values, preferred_element_type=F32)
    out = mixed[:rows]
    for i in range(1, len(scales)):
        out = jnp.where(masks[i], mixed[i * rows : (i + 1) * rows], out)
    return out.astype(BF16)


def attend_all(uq, uk, v, sharps, mixture, head):
    per = LANES // head
    each = sharps[0].shape[0]
    for group in range(uq.shape[1] // LANES):
        lanes = slice(group * LANES, (group + 1) * LANES)
        scales = []
        for i in range(per):
            index = group * per + i
            scales.append(sharps[index // each][index % each] * (head ** -0.5))
        mixture[:, lanes] = attend(uq[:, lanes], uk[:, lanes], v[:, lanes], scales, head)


def project(normed, weights, out, finish, wide=WIDE):
    low = 0
    for weight in weights:
        for at in range(0, weight.shape[1], wide):
            product = jnp.dot(normed, weight[:, at : at + wide], preferred_element_type=F32)
            for g in range(0, wide, LANES):
                out[:, low + g : low + g + LANES] = finish(product[:, g : g + LANES])
            low += wide


def project_out(mixture, weights, outs, arrivals=None):
    for at in range(0, weights[0].shape[1], OUT_WIDE):
        for arrival in arrivals[at // OUT_WIDE] if arrivals else ():
            arrival.wait()
        total, low = None, 0
        for weight in weights:
            high = low + weight.shape[0]
            term = jnp.dot(
                mixture[:, low:high], weight[:, at : at + OUT_WIDE], preferred_element_type=F32
            )
            total, low = term if total is None else total + term, high
        total = total.astype(BF16)
        low = 0
        for out in outs:
            out[:, at : at + OUT_WIDE] = total[low : low + out.shape[0]]
            low += out.shape[0]


def load_rows(copies, source, batch, scratch, low, chip, blocks):
    height = source.shape[1] // blocks
    waits = []
    for j in range(blocks):
        at = pl.multiple_of((chip ^ j) * height, height)
        waits.append(
            copies.start(
                source.at[batch, pl.ds(at, height), :],
                scratch.at[pl.ds(low + j * height, height), :],
            )
        )
    return waits


def only_in(sections):
    def wrap(body):
        def wrapped(config, place, *refs):
            here = place[2]
            active = here == sections[0]
            for other in sections[1:]:
                active = active | (here == other)
            pl.when(active)(lambda: body(config, place, *refs))

        return wrapped

    return wrap


def give_rows(raw, outs):
    low = 0
    for out in outs:
        out[...] = raw[low : low + out.shape[0], :]
        low += out.shape[0]


def first_kernel(config, place, sharp, gain, source, wq, wk, wv, wo, own_ref, other_ref, *refs):
    residuals, refs = refs[:-11], refs[-11:]
    raw, rows, wq_s, wk_s, wv_s, wo_s, uq, uk, v, mixture, sems = refs
    head, blocks, length, _ = config
    copies = Copies(sems)
    chip, core = place[0], place[1]
    waits = load_rows(copies, source, core, raw, 0, chip, blocks)
    waits += load_rows(copies, source, 1 - core, raw, length, chip, blocks)
    weights = [copies.start(w, s) for w, s in ((wq, wq_s), (wk, wk_s), (wv, wv_s))]
    arrivals = stream_out(copies, ((wo, wo_s),))
    for wait in waits:
        wait.wait()
    give_rows(raw, residuals)
    normalize_rows(raw, rows, gain)
    normed = rows[...]
    wide = wq.shape[1]
    weights[0].wait()
    project(normed, (wq_s,), uq, lambda x: unit(x, head), wide)
    weights[1].wait()
    project(normed, (wk_s,), uk, lambda x: unit(x, head), wide)
    weights[2].wait()
    project(normed, (wv_s,), v, lambda x: x.astype(BF16), wide)
    for low in (0, length):
        at = pl.ds(low, length)
        attend_all(uq[at, :], uk[at, :], v[at, :], (sharp,), mixture.at[at], head)
    project_out(mixture[...], (wo_s,), (own_ref, other_ref), arrivals)


def join_kernel(config, place, own, other, *outs):
    low = 0
    for out in outs:
        at = pl.ds(low, out.shape[0])
        out[...] = (own[at, :].astype(F32) + other[at, :].astype(F32)).astype(BF16)
        low += out.shape[0]


def finish_kernel(config, place, *refs):
    terms, out = refs[:-1], refs[-1]
    total = terms[0][...].astype(F32)
    for term in terms[1:]:
        total = total + term[...].astype(F32)
    out[...] = total.astype(BF16)


def join_halves_kernel(config, place, residual, *refs):
    terms, out = refs[:-1], refs[-1]
    each, height = len(terms) // 2, terms[0].shape[0]
    for half in range(2):
        at = pl.ds(half * height, height)
        total = residual[at, :].astype(F32)
        for term in terms[half * each : (half + 1) * each]:
            total = total + term[...].astype(F32)
        out[at, :] = total.astype(BF16)


def stream_out(copies, pairs):
    arrivals = []
    for at in range(0, pairs[0][0].shape[1], OUT_WIDE):
        columns = pl.ds(at, OUT_WIDE)
        arrivals.append(
            [copies.start(source.at[:, columns], scratch.at[:, columns]) for source, scratch in pairs]
        )
    return arrivals


def query_kernel(config, place, gain, source, wq, own_ref, other_ref, *refs):
    residuals, (raw, rows, wq_s, uq, sems) = refs[:-5], refs[-5:]
    head, blocks, length, _ = config
    copies = Copies(sems)
    chip, core = place[0], place[1]
    waits = load_rows(copies, source, core, raw, 0, chip, blocks)
    waits += load_rows(copies, source, 1 - core, raw, length, chip, blocks)
    arrival = copies.start(wq, wq_s)
    for wait in waits:
        wait.wait()
    give_rows(raw, residuals)
    normalize_rows(raw, rows, gain)
    arrival.wait()
    project(rows[...], (wq_s,), uq, lambda x: unit(x, head), wq.shape[1])
    own_ref[...] = uq[:length, :]
    other_ref[...] = uq[length:, :]


def memory_kernel(config, place, gain, *refs):
    head = config[0]
    pieces, (wk_own, wk_other, wv_own, wv_other, uk_ref, v_ref, rows) = refs[:-7], refs[-7:]
    normalize_pieces(pieces, rows, gain)
    normed = rows[...]
    project(normed, (wk_own, wk_other), uk_ref, lambda x: unit(x, head))
    project(normed, (wv_own, wv_other), v_ref, lambda x: x.astype(BF16))


def keep_kernel(config, place, *refs):
    sems, refs = refs[-1], refs[:-1]
    count = len(refs) // 2
    copies = Copies(sems)
    for wait in [copies.start(refs[i], refs[count + i]) for i in range(count)]:
        wait.wait()
    refs[-1][...] = jnp.zeros_like(refs[-1])


def mix_kernel(config, place, sharp_own, sharp_other, uq_own, uq_other, uk, v, *refs):
    wo_own, wo_other, outs, (uq, mixture) = refs[0], refs[1], refs[2:-2], refs[-2:]
    inner = uq_own.shape[1]
    uq[:, :inner] = uq_own[...]
    uq[:, inner:] = uq_other[...]
    attend_all(uq, uk, v, (sharp_own, sharp_other), mixture, config[0])
    project_out(mixture[...], (wo_own, wo_other), outs)


def pass_kernel(share, mark, out):
    out[...] = share[...]


def section_kernel(config, place, sharp_own, sharp_other, gain, *refs):
    head, _, _, count = config
    pieces, refs = refs[:count], refs[count:]
    uk, v, wq_own, wq_other, wo_own, wo_other = refs[:6]
    outs, (rows, uq, mixture) = refs[6:-3], refs[-3:]
    normalize_pieces(pieces, rows, gain)
    project(rows[...], (wq_own, wq_other), uq, lambda x: unit(x, head))
    attend_all(uq, uk, v, (sharp_own, sharp_other), mixture, head)
    project_out(mixture[...], (wo_own, wo_other), outs)


def place_kernel(config, place, *refs):
    _, blocks, _, count = config
    pieces, out = refs[:-1], refs[-1]
    chip, core = place[0], place[1]
    groups = count // blocks
    for i, piece in enumerate(pieces):
        height = piece.shape[0]
        batch = core if i < count else 1 - core
        j, g = (i % count) // groups, i % groups
        at = pl.multiple_of(((chip ^ j) * groups + g) * height, height)
        out[batch, pl.ds(at, height), :] = piece[...]


def shards(
    inbound_embedding_batches,
    decoder_embedding_batches,
    asking_projections,
    probe_projections,
    payload_projections,
    exit_projections,
    layer_rescale_weights,
    logit_sharpness,
    last_rescale_weights,
):
    sections = lax.axis_size("section")
    seq = lax.axis_size("seq")
    section = lax.axis_index("section")
    position = lax.axis_index("seq")
    encoders = 3 * sections // 8
    batches, length, width = inbound_embedding_batches.shape
    cores = 2
    blocks = seq // cores
    assert batches == cores and blocks & (blocks - 1) == 0
    core, chip = position % cores, position // cores
    height = length // blocks
    groups = 2 if height % 32 == 0 else 1
    piece = height // groups
    heads = logit_sharpness.shape[1]
    inner = asking_projections.shape[2]
    head = inner // heads
    both = cores * inner
    count = blocks * groups
    config = (head, blocks, length, count)

    def flip(bits):
        pairs = [(i, i ^ bits) for i in range(seq)]
        return lambda x: lax.ppermute(x, "seq", pairs)

    def up(x, source, target):
        return lax.ppermute(x, "section", [(source, target)])

    to_core = flip(1)
    to_chip = [None] + [flip(j * cores) for j in range(1, blocks)]

    wq, wk, wv, wo = (
        w[0] for w in (asking_projections, probe_projections, payload_projections, exit_projections)
    )
    gain = layer_rescale_weights
    last_gain = last_rescale_weights.reshape(1, width)
    sharp = logit_sharpness[0]
    sharp_other = to_core(sharp)
    stay = pltpu.with_memory_space_constraint

    place = jnp.stack([chip, core, section]).astype(jnp.int32)

    def sds(shape, dtype=BF16):
        return jax.ShapeDtypeStruct(shape, dtype)

    row_scratch = pltpu.VMEM((length, width), BF16)
    out_weight = pltpu.VMEM((inner, width), BF16)
    both_scratch = pltpu.VMEM((length, both), BF16)
    chunks = pltpu.VMEM((inner // WIDE, width, WIDE), BF16)
    partials = [sds((piece, width))] * count

    def sems(n):
        return pltpu.SemaphoreType.DMA((n,))

    def gather(shares):
        if blocks == 4 and len(shares) == 2:
            first, second = shares
            x_first, y_second = to_chip[1](first), to_chip[2](second)
            y_first, x_second = to_chip[2](first), to_chip[1](second)
            by_group = [
                [first, x_first, y_first, to_chip[2](x_first)],
                [second, x_second, y_second, to_chip[1](y_second)],
            ]
        else:
            by_group = []
            for share in shares:
                others = {j: to_chip[j](share) for j in reversed(range(1, blocks))}
                by_group.append([share] + [others[j] for j in range(1, blocks)])
        return [group[j] for j in range(blocks) for group in by_group]

    def finish(parts, residuals):
        shares = []
        for g, residual in enumerate(residuals):
            arrived = [to_chip[j](parts[j * groups + g]) for j in reversed(range(1, blocks))]
            shares.append(
                kernel_call(
                    functools.partial(finish_kernel, config),
                    sds((piece, width)),
                    [IN_SMEM] + [IN_VMEM] * (blocks + 1),
                    [],
                    4,
                )(place, residual, parts[g], *arrived)
            )
        return shares

    def add(*terms):
        return kernel_call(
            functools.partial(finish_kernel, config),
            sds((piece, width)),
            [IN_SMEM] + [IN_VMEM] * len(terms),
            [],
            4,
        )(place, *terms)

    def relayed(parts):
        (own_a, own_b), (x_a, x_b), (y_a, y_b), (d_a, d_b) = (parts[i : i + 2] for i in (0, 2, 4, 6))
        through_a, through_b = to_chip[2](d_a), to_chip[1](d_b)
        far_b, far_a = to_chip[1](x_b), to_chip[2](y_a)
        near_a, near_b = to_chip[1](add(x_a, through_a)), to_chip[2](add(y_b, through_b))
        return [own_a, far_a, near_a], [own_b, far_b, near_b]

    two_ways = blocks == 4 and groups == 2

    def finish_whole(parts, residual):
        if two_ways:
            terms = relayed(parts)
            return kernel_call(
                functools.partial(join_halves_kernel, config),
                sds((height, width)),
                [IN_SMEM] + [IN_VMEM] * 7,
                [],
                6,
            )(place, residual, *terms[0], *terms[1])
        arrived = [to_chip[j](parts[j]) for j in range(1, blocks)]
        return kernel_call(
            functools.partial(finish_kernel, config),
            sds((height, width)),
            [IN_SMEM] + [IN_VMEM] * (1 + blocks),
            [],
            6,
        )(place, residual, parts[0], *arrived)

    residual_shapes = [sds((piece, width))] * groups

    def zeros(shapes):
        return [jnp.zeros(x.shape, x.dtype) for x in shapes]

    def choose(chosen, body, shapes):
        return lax.cond(chosen, lambda: list(body()), lambda: zeros(shapes))

    def first_section():
        own, other, residual = kernel_call(
            functools.partial(first_kernel, config),
            [sds((length, width))] * 2 + [sds((height, width))],
            [IN_SMEM, IN_SMEM, IN_VMEM] + [IN_HBM] * 5,
            [pltpu.VMEM((batches * length, width), BF16)] * 2
            + [pltpu.VMEM((width, inner), BF16)] * 3
            + [out_weight]
            + [pltpu.VMEM((batches * length, inner), BF16)] * 4
            + [sems(batches * blocks + 3 + width // OUT_WIDE)],
            32,
        )(
            place, sharp, gain,
            *(stay(x, pltpu.HBM) for x in (inbound_embedding_batches, wq, wk, wv, wo)),
        )
        parts = kernel_call(
            functools.partial(join_kernel, config),
            partials if two_ways else [sds((height, width))] * blocks,
            [IN_SMEM] + [IN_VMEM] * 2,
            [],
            8,
        )(place, own, to_core(other))
        return [finish_whole(parts, residual)]

    def decoder_queries():
        own, other, *residuals = kernel_call(
            functools.partial(query_kernel, config),
            [sds((length, inner))] * 2 + residual_shapes,
            [IN_SMEM, IN_VMEM] + [IN_HBM] * 2,
            [pltpu.VMEM((batches * length, width), BF16)] * 2
            + [pltpu.VMEM((width, inner), BF16), pltpu.VMEM((batches * length, inner), BF16)]
            + [sems(batches * blocks + 1)],
            20,
        )(place, gain, *(stay(x, pltpu.HBM) for x in (decoder_embedding_batches, wq)))
        return [own, to_core(other), *residuals]

    def exchange():
        return [to_core(w) for w in (wk, wv, wo, wq)]

    def no_exchange():
        arrays = [wk, wv, wo, wq] + query_shapes
        return list(
            pl.pallas_call(
                lambda *refs: None,
                out_shape=[pltpu.HBM(x.shape, x.dtype) for x in arrays],
                out_specs=[IN_HBM] * len(arrays),
            )()
        )

    share_shape = [sds((height, width))]
    query_shapes = [sds((length, inner))] * 2 + residual_shapes
    whole, wk_other, wv_other, wo_other, wq_other, queries_own, queries_other, *target_residuals = lax.switch(
        jnp.where(section == 0, 0, jnp.where(section == encoders, 1, 2)),
        [
            lambda: first_section() + no_exchange(),
            lambda: zeros(share_shape) + exchange() + decoder_queries(),
            lambda: zeros(share_shape) + exchange() + zeros(query_shapes),
        ],
    )
    kept = whole

    def keep(arrays, after, users=None):
        _, at_place = lax.optimization_barrier((after, place))
        body = keep_kernel if users is None else only_in(users)(keep_kernel)
        return kernel_call(
            functools.partial(body, config),
            [pltpu.VMEM(x.shape, BF16) for x in arrays] + [sds((8, LANES))],
            [IN_SMEM] + [IN_HBM] * len(arrays),
            [sems(len(arrays))],
            2,
            moved=4 * len(arrays) * width * inner,
        )(at_place, *(stay(x, pltpu.HBM) for x in arrays))

    def project_memory(pieces, scale, kv):
        return kernel_call(
            functools.partial(memory_kernel, config),
            [sds((length, both))] * 2,
            [IN_SMEM] + [IN_VMEM] * (1 + len(pieces) + 4),
            [row_scratch],
            10,
        )(place, scale, *pieces, *kv)

    def first_decoder(memory):
        *near, _ = keep((wk, wk_other, wv, wv_other, wo, wo_other), memory)
        keys_values = list(project_memory(gather([memory]), last_gain, near[:4]))
        parts = kernel_call(
            functools.partial(mix_kernel, config),
            partials,
            [IN_SMEM] * 3 + [IN_VMEM] * 6,
            [both_scratch, both_scratch],
            12,
        )(place, sharp, sharp_other, queries_own, queries_other, *keys_values, *near[4:])
        return keys_values + finish(parts, target_residuals)

    def other_sections(share):
        arrived = {target: up(share, encoders - 1, target) for target in range(encoders + 1, sections)}
        memory = arrived[sections - 1]
        for target in reversed(range(encoders + 1, sections - 1)):
            memory = jnp.where(section == target, arrived[target], memory)
        *near, _ = keep((wk, wk_other, wv, wv_other), memory)
        keys_values = list(project_memory(gather([memory]), last_gain, near))
        return keys_values + zeros(residual_shapes)

    def halves(share):
        return [share[g * piece : (g + 1) * piece] for g in range(groups)]

    kept = halves(kept)
    shares = kept
    unit_keys = whole
    for step in range(1, sections):
        if step == encoders:
            if step > 1:
                whole = jnp.concatenate(shares)
            memory = up(whole, step - 1, step)
            unit_keys, values, *shares = lax.cond(
                section == step,
                functools.partial(first_decoder, memory),
                functools.partial(other_sections, whole),
            )
        else:
            if step in (1, encoders + 1):
                *near, mark = keep((wq, wq_other, wo, wo_other), unit_keys, range(step, sections))
                shares[-1] = kernel_call(
                    pass_kernel, sds((piece, width)), [IN_VMEM] * 2, [], 4
                )(shares[-1], mark)
            residuals = [up(share, step - 1, step) for share in shares]
            pieces = gather(residuals)
            if step < encoders:
                *kv, _ = keep((wk, wk_other, wv, wv_other), residuals)
                unit_keys, values = project_memory(pieces, gain, kv)
            parts = kernel_call(
                functools.partial(only_in([step])(section_kernel), config),
                partials,
                [IN_SMEM] * 3 + [IN_VMEM] * (1 + count + 6),
                [row_scratch, both_scratch, both_scratch],
                10,
            )(place, sharp, sharp_other, gain, *pieces, unit_keys, values, *near)
            shares = finish(parts, residuals)
        kept = [jnp.where(section == step, share, old) for share, old in zip(shares, kept)]

    pieces = gather(kept)
    pieces = pieces + [to_core(x) for x in pieces]
    finished = kernel_call(
        functools.partial(place_kernel, config),
        sds((batches, length, width)),
        [IN_SMEM] + [IN_VMEM] * len(pieces),
        [],
        8,
    )(place, *pieces)
    return finished[None]


def solution(mesh):
    return jax.shard_map(
        shards,
        mesh=mesh,
        in_specs=(
            P(),
            P(),
            P("section", None, "seq"),
            P("section", None, "seq"),
            P("section", None, "seq"),
            P("section", "seq", None),
            P("section", None),
            P("section", "seq"),
            P(),
        ),
        out_specs=P("section", None, None, None),
        check_vma=False,
    )
```

```python
import functools

import jax
import jax.numpy as jnp
from jax import lax
from jax.experimental import pallas as pl
from jax.experimental.pallas import tpu as pltpu
from jax.sharding import PartitionSpec as P

EPSILON = 1e-06
LANES = 128
WIDE = 256
OUT_WIDE = 1024
STEP = 16
BF16 = jnp.bfloat16
F32 = jnp.float32
MIB = 1024 * 1024
ANY = pl.BlockSpec(memory_space=pl.ANY)
IN_HBM = pl.BlockSpec(memory_space=pltpu.HBM)
IN_VMEM = pl.BlockSpec(memory_space=pltpu.VMEM)
IN_SMEM = pl.BlockSpec(memory_space=pltpu.SMEM)


def kernel_call(body, outs, ins, scratch, vmem, flops=0, moved=0):
    return pl.pallas_call(
        body,
        out_shape=outs,
        in_specs=ins,
        out_specs=jax.tree.map(lambda _: IN_VMEM, outs),
        scratch_shapes=scratch,
        compiler_params=pltpu.CompilerParams(vmem_limit_bytes=vmem * MIB),
        cost_estimate=pl.CostEstimate(flops=flops, bytes_accessed=moved, transcendentals=0),
    )


class Copies:
    def __init__(self, sems):
        self.sems, self.used = sems, 0

    def start(self, src, dst):
        copy = pltpu.make_async_copy(src, dst, self.sems.at[self.used])
        self.used += 1
        copy.start()
        return copy


def normalize(values, gain):
    values = values.astype(F32)
    factor = lax.rsqrt(jnp.mean(values * values, axis=-1, keepdims=True) + EPSILON)
    return (values * factor * gain).astype(BF16)


def normalize_rows(raw, out, gain):
    def body(i, _):
        at = pl.ds(pl.multiple_of(i * STEP, STEP), STEP)
        out[at, :] = normalize(raw[at, :], gain[...])
        return 0

    lax.fori_loop(0, raw.shape[0] // STEP, body, 0)


def normalize_pieces(pieces, out, gain):
    low = 0
    for piece in pieces:
        height = piece.shape[0]
        out[low : low + height, :] = normalize(piece[...], gain[...])
        low += height


def lane_masks(rows, head):
    lane = lax.broadcasted_iota(jnp.int32, (rows, LANES), 1)
    return [(lane // head) == i for i in range(LANES // head)]


def unit(block, head):
    masks = lane_masks(block.shape[0], head)
    squares = block * block
    factor = None
    for mask in masks:
        total = jnp.sum(jnp.where(mask, squares, 0.0), axis=-1, keepdims=True)
        own = lax.rsqrt(total / head + EPSILON)
        factor = own if factor is None else jnp.where(mask, own, factor)
    return (block * factor).astype(BF16)


def attend(queries, keys, values, scales, head):
    rows = queries.shape[0]
    masks = lane_masks(rows, head)
    stacked = jnp.concatenate(
        [jnp.where(mask, queries, jnp.zeros_like(queries)) for mask in masks], axis=0
    )
    scores = lax.dot_general(
        stacked, keys, (((1,), (1,)), ((), ())), preferred_element_type=F32
    )
    weights = []
    for i, scale in enumerate(scales):
        raised = jnp.exp(scores[i * rows : (i + 1) * rows] * scale)
        weights.append((raised / jnp.sum(raised, axis=-1, keepdims=True)).astype(BF16))
    mixed = jnp.dot(jnp.concatenate(weights, axis=0), values, preferred_element_type=F32)
    out = mixed[:rows]
    for i in range(1, len(scales)):
        out = jnp.where(masks[i], mixed[i * rows : (i + 1) * rows], out)
    return out.astype(BF16)


def attend_all(uq, uk, v, sharps, mixture, head):
    per = LANES // head
    each = sharps[0].shape[0]
    for group in range(uq.shape[1] // LANES):
        lanes = slice(group * LANES, (group + 1) * LANES)
        scales = []
        for i in range(per):
            index = group * per + i
            scales.append(sharps[index // each][index % each] * (head ** -0.5))
        mixture[:, lanes] = attend(uq[:, lanes], uk[:, lanes], v[:, lanes], scales, head)


def project(normed, weights, out, finish, wide=WIDE):
    low = 0
    for weight in weights:
        for at in range(0, weight.shape[1], wide):
            product = jnp.dot(normed, weight[:, at : at + wide], preferred_element_type=F32)
            for g in range(0, wide, LANES):
                out[:, low + g : low + g + LANES] = finish(product[:, g : g + LANES])
            low += wide


def project_out(mixture, weights, outs, arrivals=None):
    for at in range(0, weights[0].shape[1], OUT_WIDE):
        for arrival in arrivals[at // OUT_WIDE] if arrivals else ():
            arrival.wait()
        total, low = None, 0
        for weight in weights:
            high = low + weight.shape[0]
            term = jnp.dot(
                mixture[:, low:high], weight[:, at : at + OUT_WIDE], preferred_element_type=F32
            )
            total, low = term if total is None else total + term, high
        total = total.astype(BF16)
        low = 0
        for out in outs:
            out[:, at : at + OUT_WIDE] = total[low : low + out.shape[0]]
            low += out.shape[0]


def load_rows(copies, source, batch, scratch, low, chip, blocks):
    height = source.shape[1] // blocks
    waits = []
    for j in range(blocks):
        at = pl.multiple_of((chip ^ j) * height, height)
        waits.append(
            copies.start(
                source.at[batch, pl.ds(at, height), :],
                scratch.at[pl.ds(low + j * height, height), :],
            )
        )
    return waits


def only_in(sections):
    def wrap(body):
        def wrapped(config, place, *refs):
            here = place[2]
            active = here == sections[0]
            for other in sections[1:]:
                active = active | (here == other)
            pl.when(active)(lambda: body(config, place, *refs))

        return wrapped

    return wrap


def give_rows(raw, outs):
    low = 0
    for out in outs:
        out[...] = raw[low : low + out.shape[0], :]
        low += out.shape[0]


def first_kernel(config, place, sharp, gain, source, wq, wk, wv, wo, own_ref, other_ref, *refs):
    residuals, refs = refs[:-11], refs[-11:]
    raw, rows, wq_s, wk_s, wv_s, wo_s, uq, uk, v, mixture, sems = refs
    head, blocks, length, _ = config
    copies = Copies(sems)
    chip, core = place[0], place[1]
    waits = load_rows(copies, source, core, raw, 0, chip, blocks)
    waits += load_rows(copies, source, 1 - core, raw, length, chip, blocks)
    weights = [copies.start(w, s) for w, s in ((wq, wq_s), (wk, wk_s), (wv, wv_s))]
    arrivals = stream_out(copies, ((wo, wo_s),))
    for wait in waits:
        wait.wait()
    give_rows(raw, residuals)
    normalize_rows(raw, rows, gain)
    normed = rows[...]
    wide = wq.shape[1]
    weights[0].wait()
    project(normed, (wq_s,), uq, lambda x: unit(x, head), wide)
    weights[1].wait()
    project(normed, (wk_s,), uk, lambda x: unit(x, head), wide)
    weights[2].wait()
    project(normed, (wv_s,), v, lambda x: x.astype(BF16), wide)
    for low in (0, length):
        at = pl.ds(low, length)
        attend_all(uq[at, :], uk[at, :], v[at, :], (sharp,), mixture.at[at], head)
    project_out(mixture[...], (wo_s,), (own_ref, other_ref), arrivals)


def join_kernel(config, place, own, other, *outs):
    low = 0
    for out in outs:
        at = pl.ds(low, out.shape[0])
        out[...] = (own[at, :].astype(F32) + other[at, :].astype(F32)).astype(BF16)
        low += out.shape[0]


def finish_kernel(config, place, *refs):
    terms, out = refs[:-1], refs[-1]
    total = terms[0][...].astype(F32)
    for term in terms[1:]:
        total = total + term[...].astype(F32)
    out[...] = total.astype(BF16)


def join_halves_kernel(config, place, residual, *refs):
    terms, out = refs[:-1], refs[-1]
    each, height = len(terms) // 2, terms[0].shape[0]
    for half in range(2):
        at = pl.ds(half * height, height)
        total = residual[at, :].astype(F32)
        for term in terms[half * each : (half + 1) * each]:
            total = total + term[...].astype(F32)
        out[at, :] = total.astype(BF16)


def stream_out(copies, pairs):
    arrivals = []
    for at in range(0, pairs[0][0].shape[1], OUT_WIDE):
        columns = pl.ds(at, OUT_WIDE)
        arrivals.append(
            [copies.start(source.at[:, columns], scratch.at[:, columns]) for source, scratch in pairs]
        )
    return arrivals


def query_kernel(config, place, gain, source, wq, own_ref, other_ref, *refs):
    residuals, (raw, rows, wq_s, uq, sems) = refs[:-5], refs[-5:]
    head, blocks, length, _ = config
    copies = Copies(sems)
    chip, core = place[0], place[1]
    waits = load_rows(copies, source, core, raw, 0, chip, blocks)
    waits += load_rows(copies, source, 1 - core, raw, length, chip, blocks)
    arrival = copies.start(wq, wq_s)
    for wait in waits:
        wait.wait()
    give_rows(raw, residuals)
    normalize_rows(raw, rows, gain)
    arrival.wait()
    project(rows[...], (wq_s,), uq, lambda x: unit(x, head), wq.shape[1])
    own_ref[...] = uq[:length, :]
    other_ref[...] = uq[length:, :]


def memory_kernel(config, place, gain, *refs):
    head = config[0]
    pieces, (wk_own, wk_other, wv_own, wv_other, uk_ref, v_ref, rows) = refs[:-7], refs[-7:]
    normalize_pieces(pieces, rows, gain)
    normed = rows[...]
    project(normed, (wk_own, wk_other), uk_ref, lambda x: unit(x, head))
    project(normed, (wv_own, wv_other), v_ref, lambda x: x.astype(BF16))


def keep_kernel(config, place, *refs):
    sems, refs = refs[-1], refs[:-1]
    count = len(refs) // 2
    copies = Copies(sems)
    for wait in [copies.start(refs[i], refs[count + i]) for i in range(count)]:
        wait.wait()
    refs[-1][...] = jnp.zeros_like(refs[-1])


def mix_kernel(config, place, sharp_own, sharp_other, uq_own, uq_other, uk, v, *refs):
    wo_own, wo_other, outs, (uq, mixture) = refs[0], refs[1], refs[2:-2], refs[-2:]
    inner = uq_own.shape[1]
    uq[:, :inner] = uq_own[...]
    uq[:, inner:] = uq_other[...]
    attend_all(uq, uk, v, (sharp_own, sharp_other), mixture, config[0])
    project_out(mixture[...], (wo_own, wo_other), outs)


def pass_kernel(share, mark, out):
    out[...] = share[...]


def section_kernel(config, place, sharp_own, sharp_other, gain, *refs):
    head, _, _, count = config
    pieces, refs = refs[:count], refs[count:]
    uk, v, wq_own, wq_other, wo_own, wo_other = refs[:6]
    outs, (rows, uq, mixture) = refs[6:-3], refs[-3:]
    normalize_pieces(pieces, rows, gain)
    project(rows[...], (wq_own, wq_other), uq, lambda x: unit(x, head))
    attend_all(uq, uk, v, (sharp_own, sharp_other), mixture, head)
    project_out(mixture[...], (wo_own, wo_other), outs)


def place_kernel(config, place, *refs):
    _, blocks, _, count = config
    pieces, out = refs[:-1], refs[-1]
    chip, core = place[0], place[1]
    groups = count // blocks
    for i, piece in enumerate(pieces):
        height = piece.shape[0]
        batch = core if i < count else 1 - core
        j, g = (i % count) // groups, i % groups
        at = pl.multiple_of(((chip ^ j) * groups + g) * height, height)
        out[batch, pl.ds(at, height), :] = piece[...]


def shards(
    inbound_embedding_batches,
    decoder_embedding_batches,
    asking_projections,
    probe_projections,
    payload_projections,
    exit_projections,
    layer_rescale_weights,
    logit_sharpness,
    last_rescale_weights,
):
    sections = lax.axis_size("section")
    seq = lax.axis_size("seq")
    section = lax.axis_index("section")
    position = lax.axis_index("seq")
    encoders = 3 * sections // 8
    batches, length, width = inbound_embedding_batches.shape
    cores = 2
    blocks = seq // cores
    assert batches == cores and blocks & (blocks - 1) == 0
    core, chip = position % cores, position // cores
    height = length // blocks
    groups = 2 if height % 32 == 0 else 1
    piece = height // groups
    heads = logit_sharpness.shape[1]
    inner = asking_projections.shape[2]
    head = inner // heads
    both = cores * inner
    count = blocks * groups
    config = (head, blocks, length, count)

    def flip(bits):
        pairs = [(i, i ^ bits) for i in range(seq)]
        return lambda x: lax.ppermute(x, "seq", pairs)

    def up(x, source, target):
        return lax.ppermute(x, "section", [(source, target)])

    to_core = flip(1)
    to_chip = [None] + [flip(j * cores) for j in range(1, blocks)]

    wq, wk, wv, wo = (
        w[0] for w in (asking_projections, probe_projections, payload_projections, exit_projections)
    )
    gain = layer_rescale_weights
    last_gain = last_rescale_weights.reshape(1, width)
    sharp = logit_sharpness[0]
    sharp_other = to_core(sharp)
    stay = pltpu.with_memory_space_constraint

    place = jnp.stack([chip, core, section]).astype(jnp.int32)

    def sds(shape, dtype=BF16):
        return jax.ShapeDtypeStruct(shape, dtype)

    row_scratch = pltpu.VMEM((length, width), BF16)
    out_weight = pltpu.VMEM((inner, width), BF16)
    both_scratch = pltpu.VMEM((length, both), BF16)
    chunks = pltpu.VMEM((inner // WIDE, width, WIDE), BF16)
    partials = [sds((piece, width))] * count

    def sems(n):
        return pltpu.SemaphoreType.DMA((n,))

    def gather(shares):
        if blocks == 4 and len(shares) == 2:
            first, second = shares
            x_first, y_second = to_chip[1](first), to_chip[2](second)
            y_first, x_second = to_chip[2](first), to_chip[1](second)
            by_group = [
                [first, x_first, y_first, to_chip[2](x_first)],
                [second, x_second, y_second, to_chip[1](y_second)],
            ]
        else:
            by_group = []
            for share in shares:
                others = {j: to_chip[j](share) for j in reversed(range(1, blocks))}
                by_group.append([share] + [others[j] for j in range(1, blocks)])
        return [group[j] for j in range(blocks) for group in by_group]

    def finish(parts, residuals):
        shares = []
        for g, residual in enumerate(residuals):
            arrived = [to_chip[j](parts[j * groups + g]) for j in reversed(range(1, blocks))]
            shares.append(
                kernel_call(
                    functools.partial(finish_kernel, config),
                    sds((piece, width)),
                    [IN_SMEM] + [IN_VMEM] * (blocks + 1),
                    [],
                    4,
                )(place, residual, parts[g], *arrived)
            )
        return shares

    def add(*terms):
        return kernel_call(
            functools.partial(finish_kernel, config),
            sds((piece, width)),
            [IN_SMEM] + [IN_VMEM] * len(terms),
            [],
            4,
        )(place, *terms)

    def relayed(parts):
        (own_a, own_b), (x_a, x_b), (y_a, y_b), (d_a, d_b) = (parts[i : i + 2] for i in (0, 2, 4, 6))
        through_a, through_b = to_chip[2](d_a), to_chip[1](d_b)
        far_b, far_a = to_chip[1](x_b), to_chip[2](y_a)
        near_a, near_b = to_chip[1](add(x_a, through_a)), to_chip[2](add(y_b, through_b))
        return [own_a, far_a, near_a], [own_b, far_b, near_b]

    two_ways = blocks == 4 and groups == 2

    def finish_whole(parts, residual):
        if two_ways:
            terms = relayed(parts)
            return kernel_call(
                functools.partial(join_halves_kernel, config),
                sds((height, width)),
                [IN_SMEM] + [IN_VMEM] * 7,
                [],
                6,
            )(place, residual, *terms[0], *terms[1])
        arrived = [to_chip[j](parts[j]) for j in range(1, blocks)]
        return kernel_call(
            functools.partial(finish_kernel, config),
            sds((height, width)),
            [IN_SMEM] + [IN_VMEM] * (1 + blocks),
            [],
            6,
        )(place, residual, parts[0], *arrived)

    residual_shapes = [sds((piece, width))] * groups

    def zeros(shapes):
        return [jnp.zeros(x.shape, x.dtype) for x in shapes]

    def choose(chosen, body, shapes):
        return lax.cond(chosen, lambda: list(body()), lambda: zeros(shapes))

    def first_section():
        own, other, residual = kernel_call(
            functools.partial(first_kernel, config),
            [sds((length, width))] * 2 + [sds((height, width))],
            [IN_SMEM, IN_SMEM, IN_VMEM] + [IN_HBM] * 5,
            [pltpu.VMEM((batches * length, width), BF16)] * 2
            + [pltpu.VMEM((width, inner), BF16)] * 3
            + [out_weight]
            + [pltpu.VMEM((batches * length, inner), BF16)] * 4
            + [sems(batches * blocks + 3 + width // OUT_WIDE)],
            32,
        )(
            place, sharp, gain,
            *(stay(x, pltpu.HBM) for x in (inbound_embedding_batches, wq, wk, wv, wo)),
        )
        parts = kernel_call(
            functools.partial(join_kernel, config),
            partials if two_ways else [sds((height, width))] * blocks,
            [IN_SMEM] + [IN_VMEM] * 2,
            [],
            8,
        )(place, own, to_core(other))
        return [finish_whole(parts, residual)]

    def decoder_queries():
        own, other, *residuals = kernel_call(
            functools.partial(query_kernel, config),
            [sds((length, inner))] * 2 + residual_shapes,
            [IN_SMEM, IN_VMEM] + [IN_HBM] * 2,
            [pltpu.VMEM((batches * length, width), BF16)] * 2
            + [pltpu.VMEM((width, inner), BF16), pltpu.VMEM((batches * length, inner), BF16)]
            + [sems(batches * blocks + 1)],
            20,
        )(place, gain, *(stay(x, pltpu.HBM) for x in (decoder_embedding_batches, wq)))
        return [own, to_core(other), *residuals]

    def exchange():
        return [to_core(w) for w in (wk, wv, wo, wq)]

    def no_exchange():
        arrays = [wk, wv, wo, wq] + query_shapes
        return list(
            pl.pallas_call(
                lambda *refs: None,
                out_shape=[pltpu.HBM(x.shape, x.dtype) for x in arrays],
                out_specs=[IN_HBM] * len(arrays),
            )()
        )

    share_shape = [sds((height, width))]
    query_shapes = [sds((length, inner))] * 2 + residual_shapes
    whole, wk_other, wv_other, wo_other, wq_other, queries_own, queries_other, *target_residuals = lax.switch(
        jnp.where(section == 0, 0, jnp.where(section == encoders, 1, 2)),
        [
            lambda: first_section() + no_exchange(),
            lambda: zeros(share_shape) + exchange() + decoder_queries(),
            lambda: zeros(share_shape) + exchange() + zeros(query_shapes),
        ],
    )
    kept = whole

    def keep(arrays, after, users=None):
        _, at_place = lax.optimization_barrier((after, place))
        body = keep_kernel if users is None else only_in(users)(keep_kernel)
        return kernel_call(
            functools.partial(body, config),
            [pltpu.VMEM(x.shape, BF16) for x in arrays] + [sds((8, LANES))],
            [IN_SMEM] + [IN_HBM] * len(arrays),
            [sems(len(arrays))],
            2,
            moved=4 * len(arrays) * width * inner,
        )(at_place, *(stay(x, pltpu.HBM) for x in arrays))

    def project_memory(pieces, scale, kv):
        return kernel_call(
            functools.partial(memory_kernel, config),
            [sds((length, both))] * 2,
            [IN_SMEM] + [IN_VMEM] * (1 + len(pieces) + 4),
            [row_scratch],
            10,
        )(place, scale, *pieces, *kv)

    def first_decoder(memory):
        *near, _ = keep((wk, wk_other, wv, wv_other, wo, wo_other), memory)
        keys_values = list(project_memory(gather([memory]), last_gain, near[:4]))
        parts = kernel_call(
            functools.partial(mix_kernel, config),
            partials,
            [IN_SMEM] * 3 + [IN_VMEM] * 6,
            [both_scratch, both_scratch],
            12,
        )(place, sharp, sharp_other, queries_own, queries_other, *keys_values, *near[4:])
        return keys_values + finish(parts, target_residuals)

    def other_sections(share):
        arrived = {target: up(share, encoders - 1, target) for target in range(encoders + 1, sections)}
        memory = arrived[sections - 1]
        for target in reversed(range(encoders + 1, sections - 1)):
            memory = jnp.where(section == target, arrived[target], memory)
        *near, _ = keep((wk, wk_other, wv, wv_other), memory)
        keys_values = list(project_memory(gather([memory]), last_gain, near))
        return keys_values + zeros(residual_shapes)

    def halves(share):
        return [share[g * piece : (g + 1) * piece] for g in range(groups)]

    kept = halves(kept)
    shares = kept
    unit_keys = whole
    for step in range(1, sections):
        if step == encoders:
            if step > 1:
                whole = jnp.concatenate(shares)
            memory = up(whole, step - 1, step)
            unit_keys, values, *shares = lax.cond(
                section == step,
                functools.partial(first_decoder, memory),
                functools.partial(other_sections, whole),
            )
        else:
            if step in (1, encoders + 1):
                arrays = (wq, wq_other, wo, wo_other)
                if step > encoders:
                    arrays += (unit_keys, values)
                *near, mark = keep(arrays, unit_keys, range(step, sections))
                if step > encoders:
                    *near, unit_keys, values = near
                shares[-1] = kernel_call(
                    pass_kernel, sds((piece, width)), [IN_VMEM] * 2, [], 4
                )(shares[-1], mark)
            residuals = [up(share, step - 1, step) for share in shares]
            pieces = gather(residuals)
            if step < encoders:
                *kv, _ = keep((wk, wk_other, wv, wv_other), residuals)
                unit_keys, values = project_memory(pieces, gain, kv)
            parts = kernel_call(
                functools.partial(only_in([step])(section_kernel), config),
                partials,
                [IN_SMEM] * 3 + [IN_VMEM] * (1 + count + 6),
                [row_scratch, both_scratch, both_scratch],
                10,
            )(place, sharp, sharp_other, gain, *pieces, unit_keys, values, *near)
            shares = finish(parts, residuals)
        kept = [jnp.where(section == step, share, old) for share, old in zip(shares, kept)]

    pieces = gather(kept)
    pieces = pieces + [to_core(x) for x in pieces]
    finished = kernel_call(
        functools.partial(place_kernel, config),
        sds((batches, length, width)),
        [IN_SMEM] + [IN_VMEM] * len(pieces),
        [],
        8,
    )(place, *pieces)
    return finished[None]


def solution(mesh):
    return jax.shard_map(
        shards,
        mesh=mesh,
        in_specs=(
            P(),
            P(),
            P("section", None, "seq"),
            P("section", None, "seq"),
            P("section", None, "seq"),
            P("section", "seq", None),
            P("section", None),
            P("section", "seq"),
            P(),
        ),
        out_specs=P("section", None, None, None),
        check_vma=False,
    )
```

```python
import functools

import jax
import jax.numpy as jnp
from jax import lax
from jax.experimental import pallas as pl
from jax.experimental.pallas import tpu as pltpu
from jax.sharding import PartitionSpec as P

EPSILON = 1e-06
LANES = 128
WIDE = 256
OUT_WIDE = 1024
STEP = 16
BF16 = jnp.bfloat16
F32 = jnp.float32
MIB = 1024 * 1024
ANY = pl.BlockSpec(memory_space=pl.ANY)
IN_HBM = pl.BlockSpec(memory_space=pltpu.HBM)
IN_VMEM = pl.BlockSpec(memory_space=pltpu.VMEM)
IN_SMEM = pl.BlockSpec(memory_space=pltpu.SMEM)


def kernel_call(body, outs, ins, scratch, vmem, flops=0, moved=0):
    return pl.pallas_call(
        body,
        out_shape=outs,
        in_specs=ins,
        out_specs=jax.tree.map(lambda _: IN_VMEM, outs),
        scratch_shapes=scratch,
        compiler_params=pltpu.CompilerParams(vmem_limit_bytes=vmem * MIB),
        cost_estimate=pl.CostEstimate(flops=flops, bytes_accessed=moved, transcendentals=0),
    )


class Copies:
    def __init__(self, sems):
        self.sems, self.used = sems, 0

    def start(self, src, dst):
        copy = pltpu.make_async_copy(src, dst, self.sems.at[self.used])
        self.used += 1
        copy.start()
        return copy


def normalize(values, gain):
    values = values.astype(F32)
    factor = lax.rsqrt(jnp.mean(values * values, axis=-1, keepdims=True) + EPSILON)
    return (values * factor * gain).astype(BF16)


def normalize_rows(raw, out, gain):
    def body(i, _):
        at = pl.ds(pl.multiple_of(i * STEP, STEP), STEP)
        out[at, :] = normalize(raw[at, :], gain[...])
        return 0

    lax.fori_loop(0, raw.shape[0] // STEP, body, 0)


def normalize_pieces(pieces, out, gain):
    low = 0
    for piece in pieces:
        height = piece.shape[0]
        out[low : low + height, :] = normalize(piece[...], gain[...])
        low += height


def lane_masks(rows, head):
    lane = lax.broadcasted_iota(jnp.int32, (rows, LANES), 1)
    return [(lane // head) == i for i in range(LANES // head)]


def unit(block, head):
    masks = lane_masks(block.shape[0], head)
    squares = block * block
    factor = None
    for mask in masks:
        total = jnp.sum(jnp.where(mask, squares, 0.0), axis=-1, keepdims=True)
        own = lax.rsqrt(total / head + EPSILON)
        factor = own if factor is None else jnp.where(mask, own, factor)
    return (block * factor).astype(BF16)


def attend(queries, keys, values, scales, head):
    rows = queries.shape[0]
    masks = lane_masks(rows, head)
    stacked = jnp.concatenate(
        [jnp.where(mask, queries, jnp.zeros_like(queries)) for mask in masks], axis=0
    )
    scores = lax.dot_general(
        stacked, keys, (((1,), (1,)), ((), ())), preferred_element_type=F32
    )
    weights = []
    for i, scale in enumerate(scales):
        raised = jnp.exp(scores[i * rows : (i + 1) * rows] * scale)
        weights.append((raised / jnp.sum(raised, axis=-1, keepdims=True)).astype(BF16))
    mixed = jnp.dot(jnp.concatenate(weights, axis=0), values, preferred_element_type=F32)
    out = mixed[:rows]
    for i in range(1, len(scales)):
        out = jnp.where(masks[i], mixed[i * rows : (i + 1) * rows], out)
    return out.astype(BF16)


def attend_all(uq, uk, v, sharps, mixture, head):
    per = LANES // head
    each = sharps[0].shape[0]
    for group in range(uq.shape[1] // LANES):
        lanes = slice(group * LANES, (group + 1) * LANES)
        scales = []
        for i in range(per):
            index = group * per + i
            scales.append(sharps[index // each][index % each] * (head ** -0.5))
        mixture[:, lanes] = attend(uq[:, lanes], uk[:, lanes], v[:, lanes], scales, head)


def project(normed, weights, out, finish, wide=WIDE):
    low = 0
    for weight in weights:
        for at in range(0, weight.shape[1], wide):
            product = jnp.dot(normed, weight[:, at : at + wide], preferred_element_type=F32)
            for g in range(0, wide, LANES):
                out[:, low + g : low + g + LANES] = finish(product[:, g : g + LANES])
            low += wide


def project_out(mixture, weights, outs, arrivals=None):
    for at in range(0, weights[0].shape[1], OUT_WIDE):
        for arrival in arrivals[at // OUT_WIDE] if arrivals else ():
            arrival.wait()
        total, low = None, 0
        for weight in weights:
            high = low + weight.shape[0]
            term = jnp.dot(
                mixture[:, low:high], weight[:, at : at + OUT_WIDE], preferred_element_type=F32
            )
            total, low = term if total is None else total + term, high
        total = total.astype(BF16)
        low = 0
        for out in outs:
            out[:, at : at + OUT_WIDE] = total[low : low + out.shape[0]]
            low += out.shape[0]


def load_rows(copies, source, batch, scratch, low, chip, blocks):
    height = source.shape[1] // blocks
    waits = []
    for j in range(blocks):
        at = pl.multiple_of((chip ^ j) * height, height)
        waits.append(
            copies.start(
                source.at[batch, pl.ds(at, height), :],
                scratch.at[pl.ds(low + j * height, height), :],
            )
        )
    return waits


def only_in(sections):
    def wrap(body):
        def wrapped(config, place, *refs):
            here = place[2]
            active = here == sections[0]
            for other in sections[1:]:
                active = active | (here == other)
            pl.when(active)(lambda: body(config, place, *refs))

        return wrapped

    return wrap


def give_rows(raw, outs):
    low = 0
    for out in outs:
        out[...] = raw[low : low + out.shape[0], :]
        low += out.shape[0]


def first_kernel(config, place, sharp, gain, source, wq, wk, wv, wo, own_ref, other_ref, *refs):
    residuals, refs = refs[:-11], refs[-11:]
    raw, rows, wq_s, wk_s, wv_s, wo_s, uq, uk, v, mixture, sems = refs
    head, blocks, length, _ = config
    copies = Copies(sems)
    chip, core = place[0], place[1]
    waits = load_rows(copies, source, core, raw, 0, chip, blocks)
    waits += load_rows(copies, source, 1 - core, raw, length, chip, blocks)
    weights = [copies.start(w, s) for w, s in ((wq, wq_s), (wk, wk_s), (wv, wv_s))]
    arrivals = stream_out(copies, ((wo, wo_s),))
    for wait in waits:
        wait.wait()
    give_rows(raw, residuals)
    normalize_rows(raw, rows, gain)
    normed = rows[...]
    wide = wq.shape[1]
    weights[0].wait()
    project(normed, (wq_s,), uq, lambda x: unit(x, head), wide)
    weights[1].wait()
    project(normed, (wk_s,), uk, lambda x: unit(x, head), wide)
    weights[2].wait()
    project(normed, (wv_s,), v, lambda x: x.astype(BF16), wide)
    for low in (0, length):
        at = pl.ds(low, length)
        attend_all(uq[at, :], uk[at, :], v[at, :], (sharp,), mixture.at[at], head)
    project_out(mixture[...], (wo_s,), (own_ref, other_ref), arrivals)


def join_kernel(config, place, own, other, *outs):
    low = 0
    for out in outs:
        at = pl.ds(low, out.shape[0])
        out[...] = (own[at, :].astype(F32) + other[at, :].astype(F32)).astype(BF16)
        low += out.shape[0]


def finish_kernel(config, place, *refs):
    terms, out = refs[:-1], refs[-1]
    total = terms[0][...].astype(F32)
    for term in terms[1:]:
        total = total + term[...].astype(F32)
    out[...] = total.astype(BF16)


def join_halves_kernel(config, place, residual, *refs):
    terms, out = refs[:-1], refs[-1]
    each, height = len(terms) // 2, terms[0].shape[0]
    for half in range(2):
        at = pl.ds(half * height, height)
        total = residual[at, :].astype(F32)
        for term in terms[half * each : (half + 1) * each]:
            total = total + term[...].astype(F32)
        out[at, :] = total.astype(BF16)


def stream_out(copies, pairs):
    arrivals = []
    for at in range(0, pairs[0][0].shape[1], OUT_WIDE):
        columns = pl.ds(at, OUT_WIDE)
        arrivals.append(
            [copies.start(source.at[:, columns], scratch.at[:, columns]) for source, scratch in pairs]
        )
    return arrivals


def query_kernel(config, place, gain, source, wq, own_ref, other_ref, *refs):
    residuals, (raw, rows, wq_s, uq, sems) = refs[:-5], refs[-5:]
    head, blocks, length, _ = config
    copies = Copies(sems)
    chip, core = place[0], place[1]
    waits = load_rows(copies, source, core, raw, 0, chip, blocks)
    waits += load_rows(copies, source, 1 - core, raw, length, chip, blocks)
    arrival = copies.start(wq, wq_s)
    for wait in waits:
        wait.wait()
    give_rows(raw, residuals)
    normalize_rows(raw, rows, gain)
    arrival.wait()
    project(rows[...], (wq_s,), uq, lambda x: unit(x, head), wq.shape[1])
    own_ref[...] = uq[:length, :]
    other_ref[...] = uq[length:, :]


def memory_kernel(config, place, gain, *refs):
    head = config[0]
    pieces, (wk_own, wk_other, wv_own, wv_other, uk_ref, v_ref, rows) = refs[:-7], refs[-7:]
    normalize_pieces(pieces, rows, gain)
    normed = rows[...]
    project(normed, (wk_own, wk_other), uk_ref, lambda x: unit(x, head))
    project(normed, (wv_own, wv_other), v_ref, lambda x: x.astype(BF16))


def keep_kernel(config, place, *refs):
    sems, refs = refs[-1], refs[:-1]
    count = len(refs) // 2
    copies = Copies(sems)
    for wait in [copies.start(refs[i], refs[count + i]) for i in range(count)]:
        wait.wait()
    refs[-1][...] = jnp.zeros_like(refs[-1])


def mix_kernel(config, place, sharp_own, sharp_other, uq_own, uq_other, uk, v, *refs):
    wo_own, wo_other, outs, (uq, mixture) = refs[0], refs[1], refs[2:-2], refs[-2:]
    inner = uq_own.shape[1]
    uq[:, :inner] = uq_own[...]
    uq[:, inner:] = uq_other[...]
    attend_all(uq, uk, v, (sharp_own, sharp_other), mixture, config[0])
    project_out(mixture[...], (wo_own, wo_other), outs)


def pass_kernel(share, mark, out):
    out[...] = share[...]


def section_kernel(config, place, sharp_own, sharp_other, gain, *refs):
    head, _, _, count = config
    pieces, refs = refs[:count], refs[count:]
    uk, v, wq_own, wq_other, wo_own, wo_other = refs[:6]
    outs, (rows, uq, mixture) = refs[6:-3], refs[-3:]
    normalize_pieces(pieces, rows, gain)
    project(rows[...], (wq_own, wq_other), uq, lambda x: unit(x, head))
    attend_all(uq, uk, v, (sharp_own, sharp_other), mixture, head)
    project_out(mixture[...], (wo_own, wo_other), outs)


def place_kernel(config, place, *refs):
    _, blocks, _, count = config
    pieces, out = refs[:-1], refs[-1]
    chip, core = place[0], place[1]
    groups = count // blocks
    for i, piece in enumerate(pieces):
        height = piece.shape[0]
        batch = core if i < count else 1 - core
        j, g = (i % count) // groups, i % groups
        at = pl.multiple_of(((chip ^ j) * groups + g) * height, height)
        out[batch, pl.ds(at, height), :] = piece[...]


def shards(
    inbound_embedding_batches,
    decoder_embedding_batches,
    asking_projections,
    probe_projections,
    payload_projections,
    exit_projections,
    layer_rescale_weights,
    logit_sharpness,
    last_rescale_weights,
):
    sections = lax.axis_size("section")
    seq = lax.axis_size("seq")
    section = lax.axis_index("section")
    position = lax.axis_index("seq")
    encoders = 3 * sections // 8
    batches, length, width = inbound_embedding_batches.shape
    cores = 2
    blocks = seq // cores
    assert batches == cores and blocks & (blocks - 1) == 0
    core, chip = position % cores, position // cores
    height = length // blocks
    groups = 2 if height % 32 == 0 else 1
    piece = height // groups
    heads = logit_sharpness.shape[1]
    inner = asking_projections.shape[2]
    head = inner // heads
    both = cores * inner
    count = blocks * groups
    config = (head, blocks, length, count)

    def flip(bits):
        pairs = [(i, i ^ bits) for i in range(seq)]
        return lambda x: lax.ppermute(x, "seq", pairs)

    def up(x, source, target):
        return lax.ppermute(x, "section", [(source, target)])

    to_core = flip(1)
    to_chip = [None] + [flip(j * cores) for j in range(1, blocks)]

    wq, wk, wv, wo = (
        w[0] for w in (asking_projections, probe_projections, payload_projections, exit_projections)
    )
    gain = layer_rescale_weights
    last_gain = last_rescale_weights.reshape(1, width)
    sharp = logit_sharpness[0]
    sharp_other = to_core(sharp)
    stay = pltpu.with_memory_space_constraint

    place = jnp.stack([chip, core, section]).astype(jnp.int32)

    def sds(shape, dtype=BF16):
        return jax.ShapeDtypeStruct(shape, dtype)

    row_scratch = pltpu.VMEM((length, width), BF16)
    out_weight = pltpu.VMEM((inner, width), BF16)
    both_scratch = pltpu.VMEM((length, both), BF16)
    chunks = pltpu.VMEM((inner // WIDE, width, WIDE), BF16)
    partials = [sds((piece, width))] * count

    def sems(n):
        return pltpu.SemaphoreType.DMA((n,))

    def gather(shares):
        if blocks == 4 and len(shares) == 2:
            first, second = shares
            x_first, y_first = to_chip[1](first), to_chip[2](first)
            y_second, x_second = to_chip[2](second), to_chip[1](second)
            by_group = [
                [first, x_first, y_first, to_chip[2](x_first)],
                [second, x_second, y_second, to_chip[1](y_second)],
            ]
        else:
            by_group = []
            for share in shares:
                others = {j: to_chip[j](share) for j in reversed(range(1, blocks))}
                by_group.append([share] + [others[j] for j in range(1, blocks)])
        return [group[j] for j in range(blocks) for group in by_group]

    def finish(parts, residuals):
        shares = []
        for g, residual in enumerate(residuals):
            arrived = [to_chip[j](parts[j * groups + g]) for j in reversed(range(1, blocks))]
            shares.append(
                kernel_call(
                    functools.partial(finish_kernel, config),
                    sds((piece, width)),
                    [IN_SMEM] + [IN_VMEM] * (blocks + 1),
                    [],
                    4,
                )(place, residual, parts[g], *arrived)
            )
        return shares

    def add(*terms):
        return kernel_call(
            functools.partial(finish_kernel, config),
            sds((piece, width)),
            [IN_SMEM] + [IN_VMEM] * len(terms),
            [],
            4,
        )(place, *terms)

    def relayed(parts):
        (own_a, own_b), (x_a, x_b), (y_a, y_b), (d_a, d_b) = (parts[i : i + 2] for i in (0, 2, 4, 6))
        through_a, through_b = to_chip[2](d_a), to_chip[1](d_b)
        far_b, far_a = to_chip[1](x_b), to_chip[2](y_a)
        near_a, near_b = to_chip[1](add(x_a, through_a)), to_chip[2](add(y_b, through_b))
        return [own_a, far_a, near_a], [own_b, far_b, near_b]

    two_ways = blocks == 4 and groups == 2

    def finish_whole(parts, residual):
        if two_ways:
            terms = relayed(parts)
            return kernel_call(
                functools.partial(join_halves_kernel, config),
                sds((height, width)),
                [IN_SMEM] + [IN_VMEM] * 7,
                [],
                6,
            )(place, residual, *terms[0], *terms[1])
        arrived = [to_chip[j](parts[j]) for j in range(1, blocks)]
        return kernel_call(
            functools.partial(finish_kernel, config),
            sds((height, width)),
            [IN_SMEM] + [IN_VMEM] * (1 + blocks),
            [],
            6,
        )(place, residual, parts[0], *arrived)

    residual_shapes = [sds((piece, width))] * groups

    def zeros(shapes):
        return [jnp.zeros(x.shape, x.dtype) for x in shapes]

    def choose(chosen, body, shapes):
        return lax.cond(chosen, lambda: list(body()), lambda: zeros(shapes))

    def first_section():
        own, other, residual = kernel_call(
            functools.partial(first_kernel, config),
            [sds((length, width))] * 2 + [sds((height, width))],
            [IN_SMEM, IN_SMEM, IN_VMEM] + [IN_HBM] * 5,
            [pltpu.VMEM((batches * length, width), BF16)] * 2
            + [pltpu.VMEM((width, inner), BF16)] * 3
            + [out_weight]
            + [pltpu.VMEM((batches * length, inner), BF16)] * 4
            + [sems(batches * blocks + 3 + width // OUT_WIDE)],
            32,
        )(
            place, sharp, gain,
            *(stay(x, pltpu.HBM) for x in (inbound_embedding_batches, wq, wk, wv, wo)),
        )
        parts = kernel_call(
            functools.partial(join_kernel, config),
            partials if two_ways else [sds((height, width))] * blocks,
            [IN_SMEM] + [IN_VMEM] * 2,
            [],
            8,
        )(place, own, to_core(other))
        return [finish_whole(parts, residual)]

    def decoder_queries():
        own, other, *residuals = kernel_call(
            functools.partial(query_kernel, config),
            [sds((length, inner))] * 2 + residual_shapes,
            [IN_SMEM, IN_VMEM] + [IN_HBM] * 2,
            [pltpu.VMEM((batches * length, width), BF16)] * 2
            + [pltpu.VMEM((width, inner), BF16), pltpu.VMEM((batches * length, inner), BF16)]
            + [sems(batches * blocks + 1)],
            20,
        )(place, gain, *(stay(x, pltpu.HBM) for x in (decoder_embedding_batches, wq)))
        return [own, to_core(other), *residuals]

    def exchange():
        return [to_core(w) for w in (wk, wv, wo, wq)]

    def no_exchange():
        arrays = [wk, wv, wo, wq] + query_shapes
        return list(
            pl.pallas_call(
                lambda *refs: None,
                out_shape=[pltpu.HBM(x.shape, x.dtype) for x in arrays],
                out_specs=[IN_HBM] * len(arrays),
            )()
        )

    share_shape = [sds((height, width))]
    query_shapes = [sds((length, inner))] * 2 + residual_shapes
    whole, wk_other, wv_other, wo_other, wq_other, queries_own, queries_other, *target_residuals = lax.switch(
        jnp.where(section == 0, 0, jnp.where(section == encoders, 1, 2)),
        [
            lambda: first_section() + no_exchange(),
            lambda: zeros(share_shape) + exchange() + decoder_queries(),
            lambda: zeros(share_shape) + exchange() + zeros(query_shapes),
        ],
    )
    kept = whole

    def keep(arrays, after, users=None):
        _, at_place = lax.optimization_barrier((after, place))
        body = keep_kernel if users is None else only_in(users)(keep_kernel)
        return kernel_call(
            functools.partial(body, config),
            [pltpu.VMEM(x.shape, BF16) for x in arrays] + [sds((8, LANES))],
            [IN_SMEM] + [IN_HBM] * len(arrays),
            [sems(len(arrays))],
            2,
            moved=4 * len(arrays) * width * inner,
        )(at_place, *(stay(x, pltpu.HBM) for x in arrays))

    def project_memory(pieces, scale, kv):
        return kernel_call(
            functools.partial(memory_kernel, config),
            [sds((length, both))] * 2,
            [IN_SMEM] + [IN_VMEM] * (1 + len(pieces) + 4),
            [row_scratch],
            10,
        )(place, scale, *pieces, *kv)

    def first_decoder(memory):
        *near, _ = keep((wk, wk_other, wv, wv_other, wo, wo_other), memory)
        keys_values = list(project_memory(gather([memory]), last_gain, near[:4]))
        parts = kernel_call(
            functools.partial(mix_kernel, config),
            partials,
            [IN_SMEM] * 3 + [IN_VMEM] * 6,
            [both_scratch, both_scratch],
            12,
        )(place, sharp, sharp_other, queries_own, queries_other, *keys_values, *near[4:])
        return keys_values + finish(parts, target_residuals)

    def other_sections(share):
        arrived = {target: up(share, encoders - 1, target) for target in range(encoders + 1, sections)}
        memory = arrived[sections - 1]
        for target in reversed(range(encoders + 1, sections - 1)):
            memory = jnp.where(section == target, arrived[target], memory)
        *near, _ = keep((wk, wk_other, wv, wv_other), memory)
        keys_values = list(project_memory(gather([memory]), last_gain, near))
        return keys_values + zeros(residual_shapes)

    def halves(share):
        return [share[g * piece : (g + 1) * piece] for g in range(groups)]

    kept = halves(kept)
    shares = kept
    unit_keys = whole
    for step in range(1, sections):
        if step == encoders:
            if step > 1:
                whole = jnp.concatenate(shares)
            memory = up(whole, step - 1, step)
            unit_keys, values, *shares = lax.cond(
                section == step,
                functools.partial(first_decoder, memory),
                functools.partial(other_sections, whole),
            )
        else:
            if step in (1, encoders + 1):
                *near, mark = keep((wq, wq_other, wo, wo_other), unit_keys, range(step, sections))
                shares[-1] = kernel_call(
                    pass_kernel, sds((piece, width)), [IN_VMEM] * 2, [], 4
                )(shares[-1], mark)
            residuals = [up(share, step - 1, step) for share in shares]
            pieces = gather(residuals)
            if step < encoders:
                *kv, _ = keep((wk, wk_other, wv, wv_other), residuals)
                unit_keys, values = project_memory(pieces, gain, kv)
            parts = kernel_call(
                functools.partial(only_in([step])(section_kernel), config),
                partials,
                [IN_SMEM] * 3 + [IN_VMEM] * (1 + count + 6),
                [row_scratch, both_scratch, both_scratch],
                10,
            )(place, sharp, sharp_other, gain, *pieces, unit_keys, values, *near)
            shares = finish(parts, residuals)
        kept = [jnp.where(section == step, share, old) for share, old in zip(shares, kept)]

    pieces = gather(kept)
    pieces = pieces + [to_core(x) for x in pieces]
    finished = kernel_call(
        functools.partial(place_kernel, config),
        sds((batches, length, width)),
        [IN_SMEM] + [IN_VMEM] * len(pieces),
        [],
        8,
    )(place, *pieces)
    return finished[None]


def solution(mesh):
    return jax.shard_map(
        shards,
        mesh=mesh,
        in_specs=(
            P(),
            P(),
            P("section", None, "seq"),
            P("section", None, "seq"),
            P("section", None, "seq"),
            P("section", "seq", None),
            P("section", None),
            P("section", "seq"),
            P(),
        ),
        out_specs=P("section", None, None, None),
        check_vma=False,
    )
```
